32 devices in a mesh: section: 2 (over y), dp: 16 (over z, x, core).
Axes of the slice: x: 2, y: 2, z: 4, core: 2. Of those that a mesh axis runs over, the one named last changes fastest.
Arguments:
- x_in: bfloat16 [2, 4096, 1536], P(None, 'dp'), may hold values from -12 to 12
- lengths: int32 [2, 16, 2], P(None, 'dp'), may hold values from 1 to 255, as said below
- norm_pre: bfloat16 [2, 1536], P('section', 'dp'), may hold values from 0.5 to 1.5
- w_in: bfloat16 [2, 1536, 6448], P('section', 'dp'), may hold values from -0.15625 to 0.15625
- conv_w: bfloat16 [2, 4, 3328], P('section', None, 'dp'), may hold values from -0.59765625 to 0.59765625
- conv_b: bfloat16 [2, 3328], P('section', 'dp'), may hold values from -0.29882812 to 0.29882812
- dt_bias: float32 [2, 48], P('section'), may hold values from -5 to -2
- a_log: float32 [2, 48], P('section'), may hold values from 0 to 2.7
- skip_scale: float32 [2, 48], P('section'), may hold values from 0.5 to 1.5
- norm_gate: bfloat16 [2, 3072], P('section', 'dp'), may hold values from 0.5 to 1.5
- w_out: bfloat16 [2, 3072, 1536], P('section', None, 'dp'), may hold values from -0.109375 to 0.109375
- cotangent: bfloat16 [2, 4096, 1536], P(None, 'dp'), may hold values from -6 to 6
Outputs:
- outputs: float32 [2, 2, 4096, 1536], P('section', None, 'dp')
- in_grad: float32 [2, 2, 4096, 1536], P('section', None, 'dp')
- grad_norm_pre: float32 [2, 1536], P('section', 'dp')
- grad_w_in: float32 [2, 1536, 6448], P('section', 'dp')
- grad_conv_w: float32 [2, 4, 3328], P('section', None, 'dp')
- grad_conv_b: float32 [2, 3328], P('section', 'dp')
- grad_dt_bias: float32 [2, 48], P('section')
- grad_a_log: float32 [2, 48], P('section')
- grad_skip: float32 [2, 48], P('section')
- grad_norm_gate: float32 [2, 3072], P('section', 'dp')
- grad_w_out: float32 [2, 3072, 1536], P('section', None, 'dp')
- rms_stats: float32 [2, 2], P('section')
The draws below stay inside these ranges and needn't reach their ends.
Inputs may be any that keep to these rules, and one draw needn't show every extreme that they name: Row [m, j] gives the lengths of the two sequences that fill slot j of micro-batch m from its first token on, back to back; the slot's tokens after them are padding. Together they cover 256 / 2 tokens or more. In every micro-batch some slot is full and holds one sequence of a single token and one of 255 tokens.
All inputs are finite; a program needn't handle non-finite values.
Results may differ from the reference program's by a relative error of at most 0.0083.
The reference program's roundings to bfloat16 on the way (of `normed_in` and `normed_out`) count: a program that leaves them out, or rounds other values in their place, can miss the bound.
Values may be sent and summed in bfloat16 or wider, within the bound.
A program may use at most 320 MiB of HBM per device.

```python
import math
import jax
import jax.numpy as jnp
from jax import lax

D = 1536
DI = 3072
H = 48
KC = 4
MB = 2
TOK_DEV = 256
IN_W = 6448
CONV_W = 3328
SLOTS = 16
TOKENS = 4096
N_SECTION = 2


def draw_x_in(key, part):
    key = jax.random.fold_in(key, 11)
    noise_key = jax.random.fold_in(key, 0)
    position = jnp.arange(TOKENS, dtype=jnp.float32)
    rising = jnp.exp(jnp.log(3.0) * position / TOKENS)[None, :, None]
    base = jax.random.truncated_normal(noise_key, -4.0, 4.0, (MB, TOKENS, D), jnp.float32)
    return (base * rising).astype(jnp.bfloat16)


def draw_lengths(key, part):
    key = jax.random.fold_in(key, 23)
    filled_key, full_key, split_key, side_key = jax.random.split(key, 4)
    filled = jax.random.randint(filled_key, (MB, SLOTS), TOK_DEV // 2, TOK_DEV + 1)
    full_slot = jax.random.randint(full_key, (MB, 1), 0, SLOTS)
    is_full = jnp.arange(SLOTS)[None, :] == full_slot
    filled = jnp.where(is_full, TOK_DEV, filled)
    leading = jax.random.randint(split_key, (MB, SLOTS), 1, filled)
    side_bit = jax.random.randint(side_key, (MB, 1), 0, 2)
    full_lead = jnp.where(side_bit == 0, 1, TOK_DEV - 1)
    leading = jnp.where(is_full, full_lead, leading)
    return jnp.stack([leading, filled - leading], axis=-1).astype(jnp.int32)


def spiked(result, stream_key, source, target, shards_of, factor):
    def block_of(dim):
        return (jnp.arange(result.shape[dim]) // (result.shape[dim] // shards_of)).reshape((-1,) + (1,) * (result.ndim - 1 - dim))

    near = jax.random.permutation(stream_key, shards_of)[block_of(target)]
    other_side = (block_of(target) + shards_of // 2) % shards_of
    return jnp.where((block_of(source) == near) | (block_of(source) == other_side), factor * result, result)


def steps_of(key, dims, shards, smallest, largest):
    gain = 1.0
    for dim, blocks in shards:
        heights = jax.random.uniform(jax.random.fold_in(jax.random.fold_in(key, 6), dim), (blocks,), jnp.float32, smallest / len(shards), largest / len(shards))
        gain = gain * jnp.repeat(jnp.exp(heights), dims[dim] // blocks).reshape((-1,) + (1,) * (len(dims) - 1 - dim))
    return gain


def gaussian(own_key, dims, width, most, cuts=(), kind=jnp.bfloat16):
    values = width * jax.random.normal(own_key, dims, jnp.float32)
    if cuts:
        values = values * steps_of(own_key, dims, cuts, -0.22, 0.18)
    return jnp.clip(values, -most, most).astype(kind)


def noise_with(stream_key, shape, spread, most, cuts, heavy, held_as=jnp.bfloat16):
    entries = spread * jax.random.normal(stream_key, shape, jnp.float32)
    if cuts:
        entries = entries * steps_of(stream_key, shape, cuts, -0.22, 0.18)
    return jnp.clip(spiked(entries, jax.random.fold_in(stream_key, 3), *heavy), -most, most).astype(held_as)


def setup_inputs(seed: int = 0) -> dict:
    splits = jax.random.split(jax.random.key(seed), 13)
    return {
        "x_in": draw_x_in(jax.random.fold_in(splits[12], 71), 0),
        "lengths": draw_lengths(jax.random.fold_in(splits[12], 71), 0),
        "norm_pre": jnp.clip(1.0 + 0.1 * jax.random.normal(splits[2], (N_SECTION, D), jnp.float32), 0.5, 1.5).astype(jnp.bfloat16),
        "w_in": gaussian(splits[3], (N_SECTION, D, IN_W), D ** -0.5, 0.15625, ((0, 2), (1, 16))),
        "conv_w": jnp.clip(jax.random.uniform(splits[4], (N_SECTION, KC, CONV_W), jnp.float32, -0.59765625, 0.59765625) * steps_of(splits[4], (N_SECTION, KC, CONV_W), ((0, 2), (2, 16)), -0.4, 0.0), -0.59765625, 0.59765625).astype(jnp.bfloat16),
        "conv_b": jnp.clip(jax.random.uniform(splits[5], (N_SECTION, CONV_W), jnp.float32, -0.29882812, 0.29882812) * steps_of(splits[5], (N_SECTION, CONV_W), ((0, 2), (1, 16)), -0.4, 0.0), -0.29882812, 0.29882812).astype(jnp.bfloat16),
        "dt_bias": jnp.clip(-5.0 + 3.0 * jax.random.uniform(splits[6], (N_SECTION, H), jnp.float32) ** steps_of(splits[6], (N_SECTION, H), ((0, 2),), -0.2, 0.2), -5.0, -2.0),
        "a_log": jnp.clip(2.7 * jax.random.uniform(splits[7], (N_SECTION, H), jnp.float32) ** steps_of(splits[7], (N_SECTION, H), ((0, 2),), -0.2, 0.2), 0.0, 2.7),
        "skip_scale": jnp.clip(0.5 + 1.0 * jax.random.uniform(splits[8], (N_SECTION, H), jnp.float32) ** steps_of(splits[8], (N_SECTION, H), ((0, 2),), -0.2, 0.2), 0.5, 1.5),
        "norm_gate": jnp.clip(1.0 + 0.1 * jax.random.normal(splits[9], (N_SECTION, DI), jnp.float32), 0.5, 1.5).astype(jnp.bfloat16),
        "w_out": gaussian(splits[10], (N_SECTION, DI, D), DI ** -0.5, 0.109375, ((0, 2), (2, 16))),
        "cotangent": noise_with(splits[11], (MB, TOKENS, D), 1.0, 6.0, ((1, 16),), (1, 2, 16, 2.0)),
    }


epsilon = 1e-05
highest = lax.Precision.HIGHEST

@jax.custom_vjp
def low(v):
    return lax.optimization_barrier(v.astype(jnp.bfloat16)).astype(jnp.float32)

@jax.custom_vjp
def low_back(v):
    return v

def low_keep(v):
    return (low(v), None)

def low_pass(kept, grad):
    return (grad,)

def back_keep(v):
    return (v, None)

def back_low(kept, grad):
    return (low(grad),)
low.defvjp(low_keep, low_pass)
low_back.defvjp(back_keep, back_low)

def prenorm(resid, gain_vec):
    return resid * lax.rsqrt(lax.optimization_barrier(jnp.mean(resid * resid, axis=-1, keepdims=True)) + epsilon) * gain_vec

def segment_info(seq_lens, row_count):
    position = jnp.arange(row_count, dtype=jnp.int32)
    first_end = seq_lens[..., 0:1]
    second_end = first_end + seq_lens[..., 1:2]
    segment = (position >= first_end).astype(jnp.int32) + (position >= second_end).astype(jnp.int32)
    return (segment, position < second_end)

def mixer_core(projected, conv_wt, conv_bias, dt_shift, decay_log, skip_gain, gate_gain, segment):
    row_count = projected.shape[0]
    inner_width = gate_gain.shape[0]
    conv_width = conv_bias.shape[0]
    state_width = (conv_width - inner_width) // 2
    head_count = dt_shift.shape[0]
    kernel_len = conv_wt.shape[0]
    gate_in = projected[:, :inner_width]
    conv_in = projected[:, inner_width:inner_width + conv_width]
    dt_raw = projected[:, inner_width + conv_width:]
    conv_sum = conv_bias + conv_wt[kernel_len - 1] * conv_in
    for lag in range(1, kernel_len):
        earlier = jnp.concatenate([jnp.zeros((lag, conv_width), conv_in.dtype), conv_in[:-lag]], axis=0)
        same_seg = jnp.concatenate([segment[:lag] < 0, segment[lag:] == segment[:-lag]])
        conv_sum = conv_sum + conv_wt[kernel_len - 1 - lag] * jnp.where(same_seg[:, None], earlier, 0.0)
    activated = jax.nn.silu(conv_sum)
    head_in = activated[:, :inner_width].reshape(row_count, head_count, -1)
    b_proj = activated[:, inner_width:inner_width + state_width]
    c_proj = activated[:, inner_width + state_width:]
    step_size = jax.nn.softplus(dt_raw + dt_shift)
    log_decay = jnp.cumsum(step_size * -jnp.exp(decay_log), axis=0).T
    position = jnp.arange(row_count)
    causal = (position[:, None] >= position[None, :]) & (segment[:, None] == segment[None, :])
    spread_gap = log_decay[:, :, None] - log_decay[:, None, :]
    decay_mat = jnp.where(causal[None], jnp.exp(jnp.where(causal[None], spread_gap, 0.0)), 0.0)
    c_dot_b = jnp.dot(c_proj, b_proj.T, precision=highest)
    mixing = decay_mat * c_dot_b[None] * step_size.T[:, None, :]
    mixed = jnp.einsum('hts,shp->thp', mixing, head_in, precision=highest) + skip_gain[:, None] * head_in
    gated = mixed.reshape(row_count, inner_width) * jax.nn.silu(gate_in)
    return prenorm(gated, gate_gain)

def layer_group(resid, seq_lens, params):
    norm_gain, w_in_f, conv_wt, conv_bias, dt_shift, decay_log, skip_gain, gate_gain, w_out_f = params
    segment, valid = segment_info(seq_lens, resid.shape[1])
    normed_in = low(prenorm(resid, norm_gain))
    projected = low_back(jnp.einsum('gld,de->gle', normed_in, w_in_f, precision=highest))
    core = jax.vmap(mixer_core, in_axes=(0, None, None, None, None, None, None, 0))
    normed_out = low(core(projected, conv_wt, conv_bias, dt_shift, decay_log, skip_gain, gate_gain, segment))
    branch = low_back(jnp.einsum('gli,id->gld', normed_out, w_out_f, precision=highest))
    valid_f = valid.astype(resid.dtype)
    sums = (jnp.sum(valid_f[..., None] * resid * resid), jnp.sum(valid_f[..., None] * branch * branch), jnp.sum(valid_f))
    return (resid + branch, sums)

def layer_all(blocks, seq_lens, params):

    def one_group(group_in):
        return layer_group(group_in[0], group_in[1], params)
    results, sums = lax.map(jax.checkpoint(one_group), (blocks, seq_lens))
    return (results, tuple((jnp.sum(part_sum) for part_sum in sums)))

def reference(x_in, lengths, norm_pre, w_in, conv_w, conv_b, dt_bias, a_log, skip_scale, norm_gate, w_out, cotangent):
    micro_count, token_count, model_width = x_in.shape
    row_count = TOK_DEV
    block_count = micro_count * token_count // row_count
    group_size = math.gcd(block_count, max(1, 4096 // row_count))
    group_count = block_count // group_size
    blocks = x_in.astype(jnp.float32).reshape(group_count, group_size, row_count, model_width)
    seq_lens = lengths.reshape(group_count, group_size, 2)
    weights = (norm_pre, w_in, conv_w, conv_b, dt_bias, a_log, skip_scale, norm_gate, w_out)
    params_one = tuple((weight_arg[0].astype(jnp.float32) for weight_arg in weights))
    params_two = tuple((weight_arg[1].astype(jnp.float32) for weight_arg in weights))

    def run_layer(resid, params):
        return layer_all(resid, seq_lens, params)
    hidden_one, pull_one, sums_one = jax.vjp(run_layer, blocks, params_one, has_aux=True)
    hidden_two, pull_two, sums_two = jax.vjp(run_layer, hidden_one, params_two, has_aux=True)
    valid = segment_info(seq_lens, row_count)[1]
    seed_grad = cotangent.astype(jnp.float32).reshape(hidden_two.shape) * valid.astype(jnp.float32)[..., None]
    grad_hidden, grads_two = pull_two(seed_grad)
    grad_input, grads_one = pull_one(grad_hidden)
    full_shape = (2, micro_count, token_count, model_width)
    outputs = jnp.stack([hidden_one, hidden_two]).reshape(full_shape)
    in_grad = jnp.stack([grad_input, grad_hidden]).reshape(full_shape)
    grad_list = [jnp.stack([lower_grad, upper_grad]) for lower_grad, upper_grad in zip(grads_one, grads_two)]

    def rms_pair(sums):
        return jnp.stack([jnp.sqrt(sums[0] / (sums[2] * model_width)), jnp.sqrt(sums[1] / (sums[2] * model_width))])
    rms_stats = jnp.stack([rms_pair(sums_one), rms_pair(sums_two)])
    return (outputs, in_grad, grad_list[0], grad_list[1], grad_list[2], grad_list[3], grad_list[4], grad_list[5], grad_list[6], grad_list[7], grad_list[8], rms_stats)
```

```python
import functools

import jax
import jax.numpy as jnp
from jax import lax
from jax.experimental import pallas as pl
from jax.experimental.pallas import tpu as pltpu
from jax.sharding import PartitionSpec as P

EPS = 1e-05
F32 = jnp.float32
BF16 = jnp.bfloat16
LANE = 128
LOG2E = 1.4426950408889634
NEG = -1e30
VMEM_LIMIT = 60 * 1024 * 1024
HIGH = lax.Precision.HIGHEST
IN_BLOCKS = 3
OUT_BLOCKS = 4
GN_BLOCKS = 4
GNI_BLOCKS = 6


def dot_nn(a, b, precision=None):
    return lax.dot_general(
        a, b, (((1,), (0,)), ((), ())), preferred_element_type=F32, precision=precision
    )


def dot_nt(a, b, precision=None):
    return lax.dot_general(
        a, b, (((1,), (1,)), ((), ())), preferred_element_type=F32, precision=precision
    )


def dot_tn(a, b, precision=None):
    return lax.dot_general(
        a, b, (((0,), (0,)), ((), ())), preferred_element_type=F32, precision=precision
    )


def sigmoid(v):
    return 1.0 / (1.0 + jnp.exp(-v))


def iota(shape, dim):
    return lax.broadcasted_iota(jnp.int32, shape, dim)


def row_sum(v):
    return jnp.sum(v, axis=1, keepdims=True)


def col_sum(v):
    return jnp.sum(v, axis=0, keepdims=True)


def segments_of(position, first_end, second_end):
    return (position >= first_end).astype(jnp.int32) + (position >= second_end).astype(jnp.int32)


def decay_terms(dt_raw, hp_ref, rows):
    z = dt_raw + hp_ref[0:1, :]
    step = jnp.maximum(z, 0.0) + jnp.log1p(jnp.exp(-jnp.abs(z)))
    below = (iota((rows, rows), 1) <= iota((rows, rows), 0)).astype(F32)
    ld = dot_nn(below, step * (hp_ref[1:2, :] * LOG2E), HIGH)
    lr = ld - jnp.log2(jnp.maximum(step, 1e-37))
    return z, step, ld, lr


def to_rows(v, out_ref, pairs):
    vt = v.T
    for p in range(pairs):
        out_ref[p, 0:2, :] = vt[2 * p : 2 * p + 2, :]


def pair_lanes(ref, p):
    return pltpu.roll(ref[...], lax.rem(LANE - 2 * p, LANE), 1)


def fwd_kernel(
    scal, x_ref, recv_ref, win_ref, wout_ref, par_ref, hp_ref, *rest
):
    (a0, a1, a2, a3, a4, a5, a6,
     nin_ref, nout_ref, out_ref, resid_ref, proj_hbm, csum_hbm, mixed_hbm, branch_ref, stat_ref,
     proj, csum, act, mixed, gated, ld_s, lr_t, cb, maskb, sem) = rest
    step = pl.program_id(0)
    rows, di, cw = gated.shape[0], gated.shape[1], csum.shape[1]
    half = rows // 2
    slot, e1, e2 = scal[1], scal[2], scal[3]
    in_cols = win_ref.shape[1]
    out_cols = wout_ref.shape[0]
    pairs = di // LANE
    copies = (
        pltpu.make_async_copy(proj, proj_hbm.at[slot], sem.at[0]),
        pltpu.make_async_copy(csum, csum_hbm.at[slot], sem.at[1]),
        pltpu.make_async_copy(mixed, mixed_hbm.at[slot], sem.at[2]),
    )

    @pl.when(step == 0)
    def _():
        u = x_ref[0].astype(F32) + recv_ref[...].astype(F32)
        q = lax.rsqrt(jnp.mean(u * u, axis=1, keepdims=True) + EPS)
        nin_ref[0] = (u * q * par_ref[7:8, : u.shape[1]]).astype(BF16)
        resid_ref[0] = u

    for i in range(IN_BLOCKS):

        @pl.when(step == i)
        def _():
            proj[:, i * in_cols : (i + 1) * in_cols] = dot_nn(nin_ref[0], win_ref[...])

    @pl.when(step == IN_BLOCKS)
    def _():
        copies[0].start()
        pos = iota((rows, LANE), 0)
        dist = pos - jnp.where(pos >= e2, e2, jnp.where(pos >= e1, e1, 0))

        def conv_tile(j, carry):
            off = pl.multiple_of(j * LANE, LANE)
            v = proj[:, pl.ds(pl.multiple_of(di + j * LANE, LANE), LANE)]
            acc = par_ref[4:5, pl.ds(off, LANE)] + par_ref[3:4, pl.ds(off, LANE)] * v
            for lag in range(1, 4):
                acc += par_ref[3 - lag : 4 - lag, pl.ds(off, LANE)] * jnp.where(
                    dist >= lag, pltpu.roll(v, lag, 0), 0.0
                )
            csum[:, pl.ds(off, LANE)] = acc
            act[:, pl.ds(off, LANE)] = acc * sigmoid(acc)
            return carry

        lax.fori_loop(0, cw // LANE, conv_tile, 0)
        copies[1].start()
        _, _, ld, lr = decay_terms(proj[:, di + cw :], hp_ref, rows)
        ld_s[...] = ld
        to_rows(lr, lr_t, pairs)
        cb[...] = dot_nt(act[:, di + LANE :], act[:, di : di + LANE], HIGH)
        rpos, cpos = iota((rows, rows), 0), iota((rows, rows), 1)
        keep = (rpos >= cpos) & (segments_of(rpos, e1, e2) == segments_of(cpos, e1, e2))
        maskb[...] = jnp.where(keep, 0.0, NEG)
        first = iota((rows, LANE), 1) < LANE // 2

        def pair(p, sq):
            off = pl.multiple_of(p * LANE, LANE)
            x = act[:, pl.ds(off, LANE)]
            ldr = pair_lanes(ld_s, p)
            y0 = jnp.zeros((half, LANE), F32)
            y1 = jnp.zeros((half, LANE), F32)
            for h in range(2):
                xm = jnp.where(first if h == 0 else ~first, x, 0.0).astype(BF16)
                lc = ldr[:, h : h + 1]
                lrow = lr_t[p, h : h + 1, :]
                m0 = jnp.exp2((lc[:half] - lrow[:, :half]) + maskb[:half, :half]) * cb[:half, :half]
                m1 = jnp.exp2((lc[half:] - lrow) + maskb[half:, :]) * cb[half:, :]
                y0 += dot_nn(m0.astype(BF16), xm[:half])
                y1 += dot_nn(m1.astype(BF16), xm)
            y = jnp.concatenate([y0, y1], axis=0) + par_ref[6:7, pl.ds(off, LANE)] * x
            mixed[:, pl.ds(off, LANE)] = y
            gate = proj[:, pl.ds(off, LANE)]
            g = y * (gate * sigmoid(gate))
            gated[:, pl.ds(off, LANE)] = g
            return sq + g * g

        sq = lax.fori_loop(0, pairs, pair, jnp.zeros((rows, LANE), F32))
        copies[2].start()
        r = lax.rsqrt(row_sum(sq) * (1.0 / di) + EPS)
        nout_ref[0] = (gated[...] * r * par_ref[5:6, :di]).astype(BF16)

    for i in range(OUT_BLOCKS):

        @pl.when(step == IN_BLOCKS + 1 + i)
        def _():
            cols = slice(i * out_cols, (i + 1) * out_cols)
            branch = dot_nt(nout_ref[0], wout_ref[...])
            u = resid_ref[0, :, cols]
            valid = iota((rows, 1), 0) < e2
            out_ref[0, :, cols] = u + branch
            branch_ref[:, cols] = branch.astype(BF16)
            usq = col_sum(row_sum(jnp.where(valid, u * u, 0.0)))
            bsq = col_sum(row_sum(jnp.where(valid, branch * branch, 0.0)))
            lane = iota((8, LANE), 1)
            part = jnp.where(lane == 0, usq, jnp.where(lane == 1, bsq, 0.0))
            if i == 0:
                stat_ref[...] = part
            else:
                stat_ref[...] += part

    @pl.when(step == IN_BLOCKS + OUT_BLOCKS)
    def _():
        for copy in copies:
            copy.wait()


def forward_step(scal, x_in, recv, w_in, w_out_t, par, hp, held):
    rows, d = recv.shape
    di = w_out_t.shape[1]
    wide = w_in.shape[1]
    cw = par.shape[1]
    in_cols, out_rows = wide // IN_BLOCKS, d // OUT_BLOCKS
    last = IN_BLOCKS + OUT_BLOCKS

    def stacked(width):
        return pl.BlockSpec((1, rows, width), lambda i, s: (s[1], 0, 0))

    any_spec = pl.BlockSpec(memory_space=pl.ANY)
    whole = lambda i, s: (0, 0)
    grid_spec = pltpu.PrefetchScalarGridSpec(
        num_scalar_prefetch=1,
        grid=(last + 1,),
        in_specs=[
            pl.BlockSpec((1, rows, d), lambda i, s: (s[0], 0, 0)),
            pl.BlockSpec((rows, d), whole),
            pl.BlockSpec((d, in_cols), lambda i, s: (0, jnp.minimum(i, IN_BLOCKS - 1))),
            pl.BlockSpec((out_rows, di), lambda i, s: (jnp.maximum(i - IN_BLOCKS - 1, 0), 0)),
            pl.BlockSpec(par.shape, whole),
            pl.BlockSpec(hp.shape, whole),
        ]
        + [any_spec] * 7,
        out_specs=[stacked(d), stacked(di), stacked(d), stacked(d)]
        + [any_spec] * 3
        + [pl.BlockSpec((rows, d), whole), pl.BlockSpec((8, LANE), whole)],
        scratch_shapes=[
            pltpu.VMEM((rows, wide), F32),
            pltpu.VMEM((rows, cw), F32),
            pltpu.VMEM((rows, cw), F32),
            pltpu.VMEM((rows, di), F32),
            pltpu.VMEM((rows, di), F32),
            pltpu.VMEM((rows, LANE), F32),
            pltpu.VMEM((di // LANE, 8, rows), F32),
            pltpu.VMEM((rows, rows), F32),
            pltpu.VMEM((rows, rows), F32),
            pltpu.SemaphoreType.DMA((3,)),
        ],
    )
    outs = pl.pallas_call(
        fwd_kernel,
        grid_spec=grid_spec,
        out_shape=[jax.ShapeDtypeStruct(v.shape, v.dtype) for v in held]
        + [jax.ShapeDtypeStruct((rows, d), BF16), jax.ShapeDtypeStruct((8, LANE), F32)],
        input_output_aliases={7 + k: k for k in range(7)},
        compiler_params=pltpu.CompilerParams(vmem_limit_bytes=VMEM_LIMIT),
        cost_estimate=pl.CostEstimate(
            flops=2 * rows * d * (wide + di), bytes_accessed=60 << 20, transcendentals=4 << 20
        ),
        name="mixer_forward",
    )(scal, x_in, recv, w_in, w_out_t, par, hp, *held)
    return outs[:7], outs[7], outs[8]


def bwd_kernel(scal, cot_ref, recv_ref, resid_ref, win_ref, wout_ref, par_ref, hp_ref, *rest):
    (proj_hbm, csum_hbm, mixed_hbm, a0, a1, a2,
     gproj_ref, gbr_ref, ing_ref, send_ref, pack_ref,
     proj, csum, mixed, gn, gni, act_bc, ld_t, lr_s, row_q, col_q, cbt, dcbt, maskb, stat, sem) = rest
    step = pl.program_id(0)
    rows, di, cw = mixed.shape[0], mixed.shape[1], csum.shape[1]
    d = gni.shape[1]
    half = rows // 2
    src, e1, e2, seeded = scal[1], scal[3], scal[4], scal[5]
    pairs = di // LANE
    gn_cols, gni_cols = wout_ref.shape[1], win_ref.shape[0]
    gate_in = pltpu.make_async_copy(
        proj_hbm.at[src, :, pl.ds(0, di)], proj.at[:, pl.ds(0, di)], sem.at[0]
    )
    mixed_in = pltpu.make_async_copy(mixed_hbm.at[src], mixed, sem.at[1])
    conv_in = pltpu.make_async_copy(
        proj_hbm.at[src, :, pl.ds(di, proj.shape[1] - di)],
        proj.at[:, pl.ds(di, proj.shape[1] - di)],
        sem.at[2],
    )
    csum_in = pltpu.make_async_copy(csum_hbm.at[src], csum, sem.at[3])

    @pl.when(step == 0)
    def _():
        for copy in (gate_in, mixed_in, csum_in, conv_in):
            copy.start()
        valid = (iota((rows, 1), 0) < e2).astype(F32) * seeded.astype(F32)
        g = cot_ref[0].astype(F32) * valid + recv_ref[...].astype(F32)
        ing_ref[0] = g
        gbr_ref[0] = g.astype(BF16)
        stat[...] = jnp.zeros_like(stat)
        pack_ref[...] = jnp.zeros_like(pack_ref)
        gate_in.wait()
        mixed_in.wait()

    for i in range(GN_BLOCKS):

        @pl.when(step == i)
        def _():
            base = i * gn_cols
            gn[:, base : base + gn_cols] = dot_nn(gbr_ref[0], wout_ref[...])

            def tile(j, carry):
                sq, cross = carry
                off = pl.multiple_of(base + j * LANE, LANE)
                gate = proj[:, pl.ds(off, LANE)]
                gated = mixed[:, pl.ds(off, LANE)] * (gate * sigmoid(gate))
                sq += gated * gated
                cross += gated * (par_ref[5:6, pl.ds(off, LANE)] * gn[:, pl.ds(off, LANE)])
                return sq, cross

            sq, cross = lax.fori_loop(0, gn_cols // LANE, tile, (stat[0], stat[1]))
            stat[0] = sq
            stat[1] = cross

    @pl.when(step == GN_BLOCKS)
    def _():
        csum_in.wait()
        conv_in.wait()
        r = lax.rsqrt(row_sum(stat[0]) * (1.0 / di) + EPS)
        rc = r * r * r * (row_sum(stat[1]) * (1.0 / di))
        stat[0] = jnp.broadcast_to(r, (rows, LANE))
        stat[1] = jnp.broadcast_to(rc, (rows, LANE))
        z, dt, ld, lr = decay_terms(proj[:, di + cw :], hp_ref, rows)
        lr_s[...] = lr
        to_rows(ld, ld_t, pairs)
        for j in range(2):
            v = csum[:, di + j * LANE : di + (j + 1) * LANE]
            act_bc[j] = v * sigmoid(v)
        cbt[...] = dot_nt(act_bc[0], act_bc[1], HIGH)
        rpos, cpos = iota((rows, rows), 0), iota((rows, rows), 1)
        keep = (rpos <= cpos) & (segments_of(rpos, e1, e2) == segments_of(cpos, e1, e2))
        maskb[...] = jnp.where(keep, 0.0, NEG)
        dcbt[...] = jnp.zeros_like(dcbt)
        col_q[...] = jnp.zeros_like(col_q)
        row_q[...] = jnp.zeros_like(row_q)
        lane = iota((rows, LANE), 1)
        first = lane < LANE // 2
        pos = iota((rows, LANE), 0)
        ahead = jnp.where(pos < e1, e1, jnp.where(pos < e2, e2, rows)) - pos

        def conv_back(dcv, off):
            here = pl.ds(off, LANE)
            v = proj[:, pl.ds(pl.multiple_of(di + off, LANE), LANE)]
            out = par_ref[3:4, here] * dcv
            pack_ref[3:4, here] = col_sum(dcv * v)
            pack_ref[4:5, here] = col_sum(dcv)
            for lag in range(1, 4):
                moved = jnp.where(ahead > lag, pltpu.roll(dcv, rows - lag, 0), 0.0)
                out += par_ref[3 - lag : 4 - lag, here] * moved
                pack_ref[3 - lag : 4 - lag, here] = col_sum(moved * v)
            gproj_ref[0, :, pl.ds(pl.multiple_of(di + off, LANE), LANE)] = out.astype(BF16)

        def pair(p, carry):
            off = pl.multiple_of(p * LANE, LANE)
            here = pl.ds(off, LANE)
            gate = proj[:, here]
            mx = mixed[:, here]
            gnt = gn[:, here]
            sg = sigmoid(gate)
            sil = gate * sg
            gated = mx * sil
            pack_ref[5:6, here] = col_sum(gated * stat[0] * gnt)
            gg = stat[0] * (par_ref[5:6, here] * gnt) - gated * stat[1]
            dy = gg * sil
            gproj_ref[0, :, here] = (gg * mx * (sg * (1.0 + gate * (1.0 - sg)))).astype(BF16)
            cs = csum[:, here]
            sc = sigmoid(cs)
            x = cs * sc
            pack_ref[6:7, here] = col_sum(dy * x)
            xb = x.astype(BF16)
            lrr = pair_lanes(lr_s, p)
            dx0 = jnp.zeros((half, LANE), F32)
            dx1 = jnp.zeros((half, LANE), F32)
            for h in range(2):
                mine = first if h == 0 else ~first
                dym = jnp.where(mine, dy, 0.0).astype(BF16)
                lc = lrr[:, h : h + 1]
                lrow = ld_t[p, h : h + 1, :]
                d0 = jnp.exp2((lrow - lc[:half]) + maskb[:half, :])
                d1 = jnp.exp2((lrow[:, half:] - lc[half:]) + maskb[half:, half:])
                t0 = dot_nt(xb[:half], dym) * d0
                t1 = dot_nt(xb[half:], dym[half:]) * d1
                dx0 += dot_nn((d0 * cbt[:half, :]).astype(BF16), dym)
                dx1 += dot_nn((d1 * cbt[half:, half:]).astype(BF16), dym[half:])
                dcbt[:half, :] += t0
                dcbt[half:, half:] += t1
                q0 = t0 * cbt[:half, :]
                q1 = t1 * cbt[half:, half:]
                row_q[p, h : h + 1, :half] = col_sum(q0[:, :half])
                row_q[p, h : h + 1, half:] = col_sum(q0[:, half:]) + col_sum(q1)
                picked = lane == 2 * p + h
                col_q[:half, :] = jnp.where(picked[:half], row_sum(q0), col_q[:half, :])
                col_q[half:, :] = jnp.where(picked[half:], row_sum(q1), col_q[half:, :])
            dx = jnp.concatenate([dx0, dx1], axis=0) + par_ref[6:7, here] * dy
            conv_back(dx * (sc * (1.0 + cs * (1.0 - sc))), off)
            return carry

        lax.fori_loop(0, pairs, pair, 0)
        dcb = dcbt[...]
        for j, grad in enumerate((dot_nn(dcb, act_bc[1], HIGH), dot_tn(dcb, act_bc[0], HIGH))):
            cs = csum[:, di + j * LANE : di + (j + 1) * LANE]
            sc = sigmoid(cs)
            conv_back(grad * (sc * (1.0 + cs * (1.0 - sc))), di + j * LANE)
        spread = jnp.concatenate(
            [row_q[p, 0:2, :] for p in range(pairs)]
            + [jnp.zeros((LANE - 2 * pairs, rows), F32)],
            axis=0,
        )
        colq = col_q[...]
        dld = spread.T - colq
        above = (iota((rows, rows), 1) >= iota((rows, rows), 0)).astype(F32)
        after = dot_nn(above, dld, HIGH)
        sz = sigmoid(z)
        ratio = jnp.where(z < -20.0, 1.0, sz / jnp.maximum(dt, 1e-37))
        neg_rate = hp_ref[1:2, :]
        ddt = jnp.where(lane < 2 * pairs, colq * ratio + neg_rate * after * sz, 0.0)
        gproj_ref[0, :, di + cw :] = ddt.astype(BF16)
        pack_ref[7:8, d : d + LANE] = col_sum(ddt)
        pack_ref[7:8, d + LANE : d + 2 * LANE] = col_sum(
            jnp.where(lane < 2 * pairs, neg_rate * dt * after, 0.0)
        )

    for i in range(GNI_BLOCKS):

        @pl.when(step == GN_BLOCKS + 1 + i)
        def _():
            gni[:, i * gni_cols : (i + 1) * gni_cols] = dot_nt(gproj_ref[0], win_ref[...])

    @pl.when(step == GN_BLOCKS + GNI_BLOCKS)
    def _():
        u = resid_ref[0]
        gi = gni[...]
        q = lax.rsqrt(jnp.mean(u * u, axis=1, keepdims=True) + EPS)
        w = par_ref[7:8, :d] * gi
        total = ing_ref[0] + q * w - u * (q * q * q * jnp.mean(u * w, axis=1, keepdims=True))
        ing_ref[0] = total
        send_ref[...] = total.astype(BF16)
        pack_ref[7:8, :d] = col_sum(u * q * gi)


def backward_step(scal, cot, recv, w_in, w_out_t, par, hp, resid, kept, held):
    rows, d = recv.shape
    di = w_out_t.shape[1]
    wide = w_in.shape[1]
    cw = par.shape[1]
    pairs = di // LANE
    gn_cols, gni_rows = di // GN_BLOCKS, d // GNI_BLOCKS
    last = GN_BLOCKS + GNI_BLOCKS

    def stacked(width, k):
        return pl.BlockSpec((1, rows, width), lambda i, s: (s[k], 0, 0))

    any_spec = pl.BlockSpec(memory_space=pl.ANY)
    whole = lambda i, s: (0, 0)
    grid_spec = pltpu.PrefetchScalarGridSpec(
        num_scalar_prefetch=1,
        grid=(last + 1,),
        in_specs=[
            stacked(d, 0),
            pl.BlockSpec((rows, d), whole),
            stacked(d, 1),
            pl.BlockSpec((gni_rows, wide), lambda i, s: (jnp.maximum(i - GN_BLOCKS - 1, 0), 0)),
            pl.BlockSpec((d, gn_cols), lambda i, s: (0, jnp.minimum(i, GN_BLOCKS - 1))),
            pl.BlockSpec(par.shape, whole),
            pl.BlockSpec(hp.shape, whole),
        ]
        + [any_spec] * 6,
        out_specs=[
            stacked(wide, 2),
            stacked(d, 2),
            stacked(d, 2),
            pl.BlockSpec((rows, d), whole),
            pl.BlockSpec((8, cw), whole),
        ],
        scratch_shapes=[
            pltpu.VMEM((rows, wide), F32),
            pltpu.VMEM((rows, cw), F32),
            pltpu.VMEM((rows, di), F32),
            pltpu.VMEM((rows, di), F32),
            pltpu.VMEM((rows, d), F32),
            pltpu.VMEM((2, rows, LANE), F32),
            pltpu.VMEM((pairs, 8, rows), F32),
            pltpu.VMEM((rows, LANE), F32),
            pltpu.VMEM((pairs, 8, rows), F32),
            pltpu.VMEM((rows, LANE), F32),
            pltpu.VMEM((rows, rows), F32),
            pltpu.VMEM((rows, rows), F32),
            pltpu.VMEM((rows, rows), F32),
            pltpu.VMEM((2, rows, LANE), F32),
            pltpu.SemaphoreType.DMA((4,)),
        ],
    )
    outs = pl.pallas_call(
        bwd_kernel,
        grid_spec=grid_spec,
        out_shape=[jax.ShapeDtypeStruct(v.shape, v.dtype) for v in held]
        + [jax.ShapeDtypeStruct((rows, d), BF16), jax.ShapeDtypeStruct((8, cw), F32)],
        input_output_aliases={11 + k: k for k in range(3)},
        compiler_params=pltpu.CompilerParams(vmem_limit_bytes=VMEM_LIMIT),
        cost_estimate=pl.CostEstimate(
            flops=2 * rows * d * (wide + di), bytes_accessed=60 << 20, transcendentals=4 << 20
        ),
        name="mixer_backward",
    )(scal, cot, recv, resid, w_in, w_out_t, par, hp, *kept, *held)
    return outs[:3], outs[3], outs[4]


def passed_along(shard, axis, by):
    length = lax.axis_size(axis)
    pairs = [(i, i + by) for i in range(length) if 0 <= i + by < length]
    return lax.ppermute(shard, axis, pairs)


def shards(
    x_in, lengths, norm_pre, w_in, conv_w, conv_b, dt_bias, a_log, skip_scale, norm_gate, w_out, cotangent
):
    section = lax.axis_index("section")
    micros, rows, d = x_in.shape
    heads = dt_bias.shape[1]
    taps = conv_w.shape[1]
    devices = lax.axis_size("dp")
    piece, wide = w_in.shape[1], w_in.shape[2]
    di = w_out.shape[1]
    cw_piece, gate_piece = conv_w.shape[2], norm_gate.shape[1]
    cw = cw_piece * devices
    pad = LANE - heads

    small = jnp.concatenate(
        [norm_pre[0], conv_b[0], norm_gate[0], conv_w[0].reshape(-1)]
    )
    small = jnp.pad(small, (0, piece * pad - small.shape[0])).reshape(piece, pad)
    gathered_in = lax.all_gather(jnp.concatenate([w_in[0], small], axis=1), "dp", axis=0, tiled=True)
    gathered_out = lax.all_gather(w_out[0].T, "dp", axis=0, tiled=True)
    tails = gathered_in[:, wide:].reshape(devices, piece * pad).astype(F32)
    ends = [0]
    for size in (piece, cw_piece, gate_piece, taps * cw_piece):
        ends.append(ends[-1] + size)
    gain_pre = tails[:, ends[0] : ends[1]].reshape(-1)
    conv_bias = tails[:, ends[1] : ends[2]].reshape(-1)
    gate_gain = tails[:, ends[2] : ends[3]].reshape(-1)
    conv_taps = tails[:, ends[3] : ends[4]].reshape(devices, taps, cw_piece)
    conv_taps = conv_taps.transpose(1, 0, 2).reshape(taps, cw)

    def wide_row(v):
        return jnp.pad(v, (0, cw - v.shape[0]))[None]

    par = jnp.concatenate(
        [
            conv_taps,
            conv_bias[None],
            wide_row(gate_gain),
            wide_row(jnp.repeat(skip_scale[0], di // heads)),
            wide_row(gain_pre),
        ],
        axis=0,
    )
    hp = jnp.pad(jnp.stack([dt_bias[0], -jnp.exp(a_log[0])]), ((0, 6), (0, pad)))

    first_end = lengths[:, 0, 0]
    second_end = first_end + lengths[:, 0, 1]
    slots = micros + 1

    def stack(width, dtype):
        return jnp.zeros((slots, rows, width), dtype)

    held = (
        stack(d, BF16), stack(di, BF16), stack(d, F32), stack(d, F32),
        stack(wide + pad, F32), stack(cw, F32), stack(di, F32),
    )
    recv = jnp.zeros((rows, d), BF16)
    stats = jnp.zeros((8, LANE), F32)
    valid_total = jnp.zeros((), F32)
    for step_no in range(micros + 1):
        micro = step_no - section
        live = (micro >= 0) & (micro < micros)
        clipped = jnp.clip(micro, 0, micros - 1)
        scal = jnp.stack(
            [clipped, jnp.where(live, clipped, micros), first_end[clipped], second_end[clipped]]
        ).astype(jnp.int32)
        held, branch, stat = forward_step(scal, x_in, recv, gathered_in, gathered_out, par, hp, held)
        stats = stats + jnp.where(live, stat, 0.0)
        valid_total = valid_total + jnp.where(live, second_end[clipped], 0).astype(F32)
        if step_no < micros:
            recv = passed_along(branch, "section", 1)
    normed_in, normed_out, outputs, resid, proj, csum, mixed = held

    back = (stack(wide + pad, BF16), stack(d, BF16), stack(d, F32))
    recv = jnp.zeros((rows, d), BF16)
    packs = None
    for step_no in range(micros + 1):
        micro = step_no - 1 + section
        live = (micro >= 0) & (micro < micros)
        clipped = jnp.clip(micro, 0, micros - 1)
        scal = jnp.stack(
            [
                clipped, clipped, jnp.where(live, clipped, micros),
                first_end[clipped], second_end[clipped], live & (section == 1),
            ]
        ).astype(jnp.int32)
        back, sent, pack = backward_step(
            scal, cotangent, recv, gathered_in, gathered_out, par, hp, resid, (proj, csum, mixed), back
        )
        packs = pack if packs is None else packs + pack
        if step_no < micros:
            recv = passed_along(sent, "section", -1)
    grad_proj, grad_branch, in_grad = back

    def joined(v):
        return v[:micros].reshape(micros * rows, v.shape[2])

    weight_out = dot_tn(joined(grad_branch), joined(normed_out)).astype(BF16)
    weight_in = dot_tn(joined(normed_in), joined(grad_proj)).astype(BF16)
    out_shard = lax.psum_scatter(weight_out, "dp", scatter_dimension=0, tiled=True).astype(F32).T
    in_shard = lax.psum_scatter(weight_in, "dp", scatter_dimension=0, tiled=True).astype(F32)[:, :wide]

    scalars = jnp.concatenate([stats[0, :2], valid_total[None]])
    packs, scalars = lax.psum((packs, scalars), "dp")
    me = lax.axis_index("dp")
    per_head = packs[6, :di].reshape(heads, di // heads).sum(axis=1)
    rms = jnp.sqrt(scalars[:2] / (scalars[2] * d))

    def mine(v, size):
        return lax.dynamic_slice_in_dim(v, me * size, size, axis=v.ndim - 1)

    return (
        outputs[:micros][None],
        in_grad[:micros][None],
        mine(packs[7, :d], piece)[None],
        in_shard[None],
        mine(packs[:taps], cw_piece)[None],
        mine(packs[4], cw_piece)[None],
        packs[7, d : d + heads][None],
        packs[7, d + LANE : d + LANE + heads][None],
        per_head[None],
        mine(packs[5, :di], gate_piece)[None],
        out_shard[None],
        rms[None],
    )


def solution(mesh):
    placed = (
        P(None, "dp", None),
        P(None, "dp", None),
        P("section", "dp"),
        P("section", "dp", None),
        P("section", None, "dp"),
        P("section", "dp"),
        P("section", None),
        P("section", None),
        P("section", None),
        P("section", "dp"),
        P("section", None, "dp"),
        P(None, "dp", None),
    )
    return jax.shard_map(
        shards,
        mesh=mesh,
        in_specs=placed,
        out_specs=(
            P("section", None, "dp", None),
            P("section", None, "dp", None),
            P("section", "dp"),
            P("section", "dp", None),
            P("section", None, "dp"),
            P("section", "dp"),
            P("section", None),
            P("section", None),
            P("section", None),
            P("section", "dp"),
            P("section", None, "dp"),
            P("section", None),
        ),
        check_vma=False,
    )
```

```python
import functools

import jax
import jax.numpy as jnp
from jax import lax
from jax.experimental import pallas as pl
from jax.experimental.pallas import tpu as pltpu
from jax.sharding import PartitionSpec as P

EPS = 1e-05
F32 = jnp.float32
BF16 = jnp.bfloat16
LANE = 128
LOG2E = 1.4426950408889634
NEG = -1e30
VMEM_LIMIT = 60 * 1024 * 1024
HIGH = lax.Precision.HIGHEST
IN_BLOCKS = 3
OUT_BLOCKS = 4
GN_BLOCKS = 4
GNI_BLOCKS = 6


def dot_nn(a, b, precision=None):
    return lax.dot_general(
        a, b, (((1,), (0,)), ((), ())), preferred_element_type=F32, precision=precision
    )


def dot_nt(a, b, precision=None):
    return lax.dot_general(
        a, b, (((1,), (1,)), ((), ())), preferred_element_type=F32, precision=precision
    )


def dot_tn(a, b, precision=None):
    return lax.dot_general(
        a, b, (((0,), (0,)), ((), ())), preferred_element_type=F32, precision=precision
    )


def sigmoid(v):
    return 1.0 / (1.0 + jnp.exp(-v))


def iota(shape, dim):
    return lax.broadcasted_iota(jnp.int32, shape, dim)


def row_sum(v):
    return jnp.sum(v, axis=1, keepdims=True)


def col_sum(v):
    return jnp.sum(v, axis=0, keepdims=True)


def segments_of(position, first_end, second_end):
    return (position >= first_end).astype(jnp.int32) + (position >= second_end).astype(jnp.int32)


def decay_terms(dt_raw, hp_ref, rows):
    z = dt_raw + hp_ref[0:1, :]
    step = jnp.maximum(z, 0.0) + jnp.log1p(jnp.exp(-jnp.abs(z)))
    below = (iota((rows, rows), 1) <= iota((rows, rows), 0)).astype(F32)
    ld = dot_nn(below, step * (hp_ref[1:2, :] * LOG2E), HIGH)
    lr = ld - jnp.log2(jnp.maximum(step, 1e-37))
    return z, step, ld, lr


def to_rows(v, out_ref, pairs):
    vt = v.T
    for p in range(pairs):
        out_ref[p, 0:2, :] = vt[2 * p : 2 * p + 2, :]


def pair_lanes(ref, p):
    return pltpu.roll(ref[...], lax.rem(LANE - 2 * p, LANE), 1)


def fwd_kernel(
    scal, x_ref, recv_ref, win_ref, wout_ref, par_ref, hp_ref, *rest
):
    (nin_ref, nout_ref, out_ref, resid_ref, proj_hbm, csum_hbm, mixed_hbm, branch_ref, stat_ref,
     proj, csum, act, mixed, gated, ld_s, lr_t, cb, maskb, sem) = rest[-19:]
    step = pl.program_id(0)
    rows, di, cw = gated.shape[0], gated.shape[1], csum.shape[1]
    half = rows // 2
    slot, e1, e2 = scal[1], scal[2], scal[3]
    in_cols = win_ref.shape[1]
    out_cols = wout_ref.shape[0]
    pairs = di // LANE
    copies = (
        pltpu.make_async_copy(proj, proj_hbm.at[slot], sem.at[0]),
        pltpu.make_async_copy(csum, csum_hbm.at[slot], sem.at[1]),
        pltpu.make_async_copy(mixed, mixed_hbm.at[slot], sem.at[2]),
    )

    @pl.when(step == 0)
    def _():
        u = x_ref[0].astype(F32) + recv_ref[...].astype(F32)
        q = lax.rsqrt(jnp.mean(u * u, axis=1, keepdims=True) + EPS)
        nin_ref[0] = (u * q * par_ref[7:8, : u.shape[1]]).astype(BF16)
        resid_ref[0] = u

    for i in range(IN_BLOCKS):

        @pl.when(step == i)
        def _():
            proj[:, i * in_cols : (i + 1) * in_cols] = dot_nn(nin_ref[0], win_ref[...])

    @pl.when(step == IN_BLOCKS)
    def _():
        copies[0].start()
        pos = iota((rows, LANE), 0)
        dist = pos - jnp.where(pos >= e2, e2, jnp.where(pos >= e1, e1, 0))

        def conv_tile(j, carry):
            off = pl.multiple_of(j * LANE, LANE)
            v = proj[:, pl.ds(pl.multiple_of(di + j * LANE, LANE), LANE)]
            acc = par_ref[4:5, pl.ds(off, LANE)] + par_ref[3:4, pl.ds(off, LANE)] * v
            for lag in range(1, 4):
                acc += par_ref[3 - lag : 4 - lag, pl.ds(off, LANE)] * jnp.where(
                    dist >= lag, pltpu.roll(v, lag, 0), 0.0
                )
            csum[:, pl.ds(off, LANE)] = acc
            act[:, pl.ds(off, LANE)] = acc * sigmoid(acc)
            return carry

        lax.fori_loop(0, cw // LANE, conv_tile, 0)
        copies[1].start()
        _, _, ld, lr = decay_terms(proj[:, di + cw :], hp_ref, rows)
        ld_s[...] = ld
        to_rows(lr, lr_t, pairs)
        cb[...] = dot_nt(act[:, di + LANE :], act[:, di : di + LANE], HIGH)
        rpos, cpos = iota((rows, rows), 0), iota((rows, rows), 1)
        keep = (rpos >= cpos) & (segments_of(rpos, e1, e2) == segments_of(cpos, e1, e2))
        maskb[...] = jnp.where(keep, 0.0, NEG)
        first = iota((rows, LANE), 1) < LANE // 2

        def pair(p, sq):
            off = pl.multiple_of(p * LANE, LANE)
            x = act[:, pl.ds(off, LANE)]
            ldr = pair_lanes(ld_s, p)
            y0 = jnp.zeros((half, LANE), F32)
            y1 = jnp.zeros((half, LANE), F32)
            for h in range(2):
                xm = jnp.where(first if h == 0 else ~first, x, 0.0).astype(BF16)
                lc = ldr[:, h : h + 1]
                lrow = lr_t[p, h : h + 1, :]
                m0 = jnp.exp2((lc[:half] - lrow[:, :half]) + maskb[:half, :half]) * cb[:half, :half]
                m1 = jnp.exp2((lc[half:] - lrow) + maskb[half:, :]) * cb[half:, :]
                y0 += dot_nn(m0.astype(BF16), xm[:half])
                y1 += dot_nn(m1.astype(BF16), xm)
            y = jnp.concatenate([y0, y1], axis=0) + par_ref[6:7, pl.ds(off, LANE)] * x
            mixed[:, pl.ds(off, LANE)] = y
            gate = proj[:, pl.ds(off, LANE)]
            g = y * (gate * sigmoid(gate))
            gated[:, pl.ds(off, LANE)] = g
            return sq + g * g

        sq = lax.fori_loop(0, pairs, pair, jnp.zeros((rows, LANE), F32))
        copies[2].start()
        r = lax.rsqrt(row_sum(sq) * (1.0 / di) + EPS)
        nout_ref[0] = (gated[...] * r * par_ref[5:6, :di]).astype(BF16)

    for i in range(OUT_BLOCKS):

        @pl.when(step == IN_BLOCKS + 1 + i)
        def _():
            cols = slice(i * out_cols, (i + 1) * out_cols)
            branch = dot_nt(nout_ref[0], wout_ref[...])
            u = resid_ref[0, :, cols]
            valid = iota((rows, 1), 0) < e2
            out_ref[0, :, cols] = u + branch
            branch_ref[:, cols] = branch.astype(BF16)
            usq = col_sum(row_sum(jnp.where(valid, u * u, 0.0)))
            bsq = col_sum(row_sum(jnp.where(valid, branch * branch, 0.0)))
            lane = iota((8, LANE), 1)
            part = jnp.where(lane == 0, usq, jnp.where(lane == 1, bsq, 0.0))
            if i == 0:
                stat_ref[...] = part
            else:
                stat_ref[...] += part

    @pl.when(step == IN_BLOCKS + OUT_BLOCKS)
    def _():
        for copy in copies:
            copy.wait()


def forward_step(scal, x_in, recv, w_in, w_out_t, par, hp, stacks, held):
    rows, d = recv.shape
    di = w_out_t.shape[1]
    wide = w_in.shape[1]
    cw = par.shape[1]
    in_cols, out_rows = wide // IN_BLOCKS, d // OUT_BLOCKS
    last = IN_BLOCKS + OUT_BLOCKS

    def stacked(width):
        return pl.BlockSpec((1, rows, width), lambda i, s: (s[1], 0, 0))

    any_spec = pl.BlockSpec(memory_space=pl.ANY)
    whole = lambda i, s: (0, 0)
    grid_spec = pltpu.PrefetchScalarGridSpec(
        num_scalar_prefetch=1,
        grid=(last + 1,),
        in_specs=[
            pl.BlockSpec((1, rows, d), lambda i, s: (s[0], 0, 0)),
            pl.BlockSpec((rows, d), whole),
            pl.BlockSpec((d, in_cols), lambda i, s: (0, jnp.minimum(i, IN_BLOCKS - 1))),
            pl.BlockSpec((out_rows, di), lambda i, s: (jnp.maximum(i - IN_BLOCKS - 1, 0), 0)),
            pl.BlockSpec(par.shape, whole),
            pl.BlockSpec(hp.shape, whole),
        ]
        + [any_spec] * len(held),
        out_specs=[stacked(d), stacked(di), stacked(d), stacked(d)]
        + [any_spec] * 3
        + [pl.BlockSpec((rows, d), whole), pl.BlockSpec((8, LANE), whole)],
        scratch_shapes=[
            pltpu.VMEM((rows, wide), F32),
            pltpu.VMEM((rows, cw), F32),
            pltpu.VMEM((rows, cw), F32),
            pltpu.VMEM((rows, di), F32),
            pltpu.VMEM((rows, di), F32),
            pltpu.VMEM((rows, LANE), F32),
            pltpu.VMEM((di // LANE, 8, rows), F32),
            pltpu.VMEM((rows, rows), F32),
            pltpu.VMEM((rows, rows), F32),
            pltpu.SemaphoreType.DMA((3,)),
        ],
    )
    outs = pl.pallas_call(
        fwd_kernel,
        grid_spec=grid_spec,
        out_shape=list(stacks)
        + [jax.ShapeDtypeStruct((rows, d), BF16), jax.ShapeDtypeStruct((8, LANE), F32)],
        input_output_aliases={7 + k: k for k in range(len(held))},
        compiler_params=pltpu.CompilerParams(vmem_limit_bytes=VMEM_LIMIT),
        cost_estimate=pl.CostEstimate(
            flops=2 * rows * d * (wide + di), bytes_accessed=60 << 20, transcendentals=4 << 20
        ),
        name="mixer_forward",
    )(scal, x_in, recv, w_in, w_out_t, par, hp, *held)
    return outs[:7], outs[7], outs[8]


def bwd_kernel(scal, cot_ref, recv_ref, resid_ref, win_ref, wout_ref, par_ref, hp_ref, *rest):
    proj_hbm, csum_hbm, mixed_hbm = rest[:3]
    (gproj_ref, gbr_ref, ing_ref, send_ref, pack_ref,
     proj, csum, mixed, gn, gni, act_bc, ld_t, lr_s, row_q, col_q, cbt, dcbt, maskb, stat, sem) = rest[-20:]
    step = pl.program_id(0)
    rows, di, cw = mixed.shape[0], mixed.shape[1], csum.shape[1]
    d = gni.shape[1]
    half = rows // 2
    src, e1, e2, seeded = scal[1], scal[3], scal[4], scal[5]
    pairs = di // LANE
    gn_cols, gni_cols = wout_ref.shape[1], win_ref.shape[0]
    gate_in = pltpu.make_async_copy(
        proj_hbm.at[src, :, pl.ds(0, di)], proj.at[:, pl.ds(0, di)], sem.at[0]
    )
    mixed_in = pltpu.make_async_copy(mixed_hbm.at[src], mixed, sem.at[1])
    conv_in = pltpu.make_async_copy(
        proj_hbm.at[src, :, pl.ds(di, proj.shape[1] - di)],
        proj.at[:, pl.ds(di, proj.shape[1] - di)],
        sem.at[2],
    )
    csum_in = pltpu.make_async_copy(csum_hbm.at[src], csum, sem.at[3])

    @pl.when(step == 0)
    def _():
        for copy in (gate_in, mixed_in, csum_in, conv_in):
            copy.start()
        valid = (iota((rows, 1), 0) < e2).astype(F32) * seeded.astype(F32)
        g = cot_ref[0].astype(F32) * valid + recv_ref[...].astype(F32)
        ing_ref[0] = g
        gbr_ref[0] = g.astype(BF16)
        stat[...] = jnp.zeros_like(stat)
        pack_ref[...] = jnp.zeros_like(pack_ref)
        gate_in.wait()
        mixed_in.wait()

    for i in range(GN_BLOCKS):

        @pl.when(step == i)
        def _():
            base = i * gn_cols
            gn[:, base : base + gn_cols] = dot_nn(gbr_ref[0], wout_ref[...])

            def tile(j, carry):
                sq, cross = carry
                off = pl.multiple_of(base + j * LANE, LANE)
                gate = proj[:, pl.ds(off, LANE)]
                gated = mixed[:, pl.ds(off, LANE)] * (gate * sigmoid(gate))
                sq += gated * gated
                cross += gated * (par_ref[5:6, pl.ds(off, LANE)] * gn[:, pl.ds(off, LANE)])
                return sq, cross

            sq, cross = lax.fori_loop(0, gn_cols // LANE, tile, (stat[0], stat[1]))
            stat[0] = sq
            stat[1] = cross

    @pl.when(step == GN_BLOCKS)
    def _():
        csum_in.wait()
        conv_in.wait()
        r = lax.rsqrt(row_sum(stat[0]) * (1.0 / di) + EPS)
        rc = r * r * r * (row_sum(stat[1]) * (1.0 / di))
        stat[0] = jnp.broadcast_to(r, (rows, LANE))
        stat[1] = jnp.broadcast_to(rc, (rows, LANE))
        z, dt, ld, lr = decay_terms(proj[:, di + cw :], hp_ref, rows)
        lr_s[...] = lr
        to_rows(ld, ld_t, pairs)
        for j in range(2):
            v = csum[:, di + j * LANE : di + (j + 1) * LANE]
            act_bc[j] = v * sigmoid(v)
        cbt[...] = dot_nt(act_bc[0], act_bc[1], HIGH)
        rpos, cpos = iota((rows, rows), 0), iota((rows, rows), 1)
        keep = (rpos <= cpos) & (segments_of(rpos, e1, e2) == segments_of(cpos, e1, e2))
        maskb[...] = jnp.where(keep, 0.0, NEG)
        dcbt[...] = jnp.zeros_like(dcbt)
        col_q[...] = jnp.zeros_like(col_q)
        row_q[...] = jnp.zeros_like(row_q)
        lane = iota((rows, LANE), 1)
        first = lane < LANE // 2
        pos = iota((rows, LANE), 0)
        ahead = jnp.where(pos < e1, e1, jnp.where(pos < e2, e2, rows)) - pos

        def conv_back(dcv, off):
            here = pl.ds(off, LANE)
            v = proj[:, pl.ds(pl.multiple_of(di + off, LANE), LANE)]
            out = par_ref[3:4, here] * dcv
            pack_ref[3:4, here] = col_sum(dcv * v)
            pack_ref[4:5, here] = col_sum(dcv)
            for lag in range(1, 4):
                moved = jnp.where(ahead > lag, pltpu.roll(dcv, rows - lag, 0), 0.0)
                out += par_ref[3 - lag : 4 - lag, here] * moved
                pack_ref[3 - lag : 4 - lag, here] = col_sum(moved * v)
            gproj_ref[0, :, pl.ds(pl.multiple_of(di + off, LANE), LANE)] = out.astype(BF16)

        def pair(p, carry):
            off = pl.multiple_of(p * LANE, LANE)
            here = pl.ds(off, LANE)
            gate = proj[:, here]
            mx = mixed[:, here]
            gnt = gn[:, here]
            sg = sigmoid(gate)
            sil = gate * sg
            gated = mx * sil
            pack_ref[5:6, here] = col_sum(gated * stat[0] * gnt)
            gg = stat[0] * (par_ref[5:6, here] * gnt) - gated * stat[1]
            dy = gg * sil
            gproj_ref[0, :, here] = (gg * mx * (sg * (1.0 + gate * (1.0 - sg)))).astype(BF16)
            cs = csum[:, here]
            sc = sigmoid(cs)
            x = cs * sc
            pack_ref[6:7, here] = col_sum(dy * x)
            xb = x.astype(BF16)
            lrr = pair_lanes(lr_s, p)
            dx0 = jnp.zeros((half, LANE), F32)
            dx1 = jnp.zeros((half, LANE), F32)
            for h in range(2):
                mine = first if h == 0 else ~first
                dym = jnp.where(mine, dy, 0.0).astype(BF16)
                lc = lrr[:, h : h + 1]
                lrow = ld_t[p, h : h + 1, :]
                d0 = jnp.exp2((lrow - lc[:half]) + maskb[:half, :])
                d1 = jnp.exp2((lrow[:, half:] - lc[half:]) + maskb[half:, half:])
                t0 = dot_nt(xb[:half], dym) * d0
                t1 = dot_nt(xb[half:], dym[half:]) * d1
                dx0 += dot_nn((d0 * cbt[:half, :]).astype(BF16), dym)
                dx1 += dot_nn((d1 * cbt[half:, half:]).astype(BF16), dym[half:])
                dcbt[:half, :] += t0
                dcbt[half:, half:] += t1
                q0 = t0 * cbt[:half, :]
                q1 = t1 * cbt[half:, half:]
                row_q[p, h : h + 1, :half] = col_sum(q0[:, :half])
                row_q[p, h : h + 1, half:] = col_sum(q0[:, half:]) + col_sum(q1)
                picked = lane == 2 * p + h
                col_q[:half, :] = jnp.where(picked[:half], row_sum(q0), col_q[:half, :])
                col_q[half:, :] = jnp.where(picked[half:], row_sum(q1), col_q[half:, :])
            dx = jnp.concatenate([dx0, dx1], axis=0) + par_ref[6:7, here] * dy
            conv_back(dx * (sc * (1.0 + cs * (1.0 - sc))), off)
            return carry

        lax.fori_loop(0, pairs, pair, 0)
        dcb = dcbt[...]
        for j, grad in enumerate((dot_nn(dcb, act_bc[1], HIGH), dot_tn(dcb, act_bc[0], HIGH))):
            cs = csum[:, di + j * LANE : di + (j + 1) * LANE]
            sc = sigmoid(cs)
            conv_back(grad * (sc * (1.0 + cs * (1.0 - sc))), di + j * LANE)
        spread = jnp.concatenate(
            [row_q[p, 0:2, :] for p in range(pairs)]
            + [jnp.zeros((LANE - 2 * pairs, rows), F32)],
            axis=0,
        )
        colq = col_q[...]
        dld = spread.T - colq
        above = (iota((rows, rows), 1) >= iota((rows, rows), 0)).astype(F32)
        after = dot_nn(above, dld, HIGH)
        sz = sigmoid(z)
        ratio = jnp.where(z < -20.0, 1.0, sz / jnp.maximum(dt, 1e-37))
        neg_rate = hp_ref[1:2, :]
        ddt = jnp.where(lane < 2 * pairs, colq * ratio + neg_rate * after * sz, 0.0)
        gproj_ref[0, :, di + cw :] = ddt.astype(BF16)
        pack_ref[7:8, d : d + LANE] = col_sum(ddt)
        pack_ref[7:8, d + LANE : d + 2 * LANE] = col_sum(
            jnp.where(lane < 2 * pairs, neg_rate * dt * after, 0.0)
        )

    for i in range(GNI_BLOCKS):

        @pl.when(step == GN_BLOCKS + 1 + i)
        def _():
            gni[:, i * gni_cols : (i + 1) * gni_cols] = dot_nt(gproj_ref[0], win_ref[...])

    @pl.when(step == GN_BLOCKS + GNI_BLOCKS)
    def _():
        u = resid_ref[0]
        gi = gni[...]
        q = lax.rsqrt(jnp.mean(u * u, axis=1, keepdims=True) + EPS)
        w = par_ref[7:8, :d] * gi
        total = ing_ref[0] + q * w - u * (q * q * q * jnp.mean(u * w, axis=1, keepdims=True))
        ing_ref[0] = total
        send_ref[...] = total.astype(BF16)
        pack_ref[7:8, :d] = col_sum(u * q * gi)


def backward_step(scal, cot, recv, w_in, w_out_t, par, hp, resid, kept, stacks, held):
    rows, d = recv.shape
    di = w_out_t.shape[1]
    wide = w_in.shape[1]
    cw = par.shape[1]
    pairs = di // LANE
    gn_cols, gni_rows = di // GN_BLOCKS, d // GNI_BLOCKS
    last = GN_BLOCKS + GNI_BLOCKS

    def stacked(width, k):
        return pl.BlockSpec((1, rows, width), lambda i, s: (s[k], 0, 0))

    any_spec = pl.BlockSpec(memory_space=pl.ANY)
    whole = lambda i, s: (0, 0)
    grid_spec = pltpu.PrefetchScalarGridSpec(
        num_scalar_prefetch=1,
        grid=(last + 1,),
        in_specs=[
            stacked(d, 0),
            pl.BlockSpec((rows, d), whole),
            stacked(d, 1),
            pl.BlockSpec((gni_rows, wide), lambda i, s: (jnp.maximum(i - GN_BLOCKS - 1, 0), 0)),
            pl.BlockSpec((d, gn_cols), lambda i, s: (0, jnp.minimum(i, GN_BLOCKS - 1))),
            pl.BlockSpec(par.shape, whole),
            pl.BlockSpec(hp.shape, whole),
        ]
        + [any_spec] * (3 + len(held)),
        out_specs=[
            stacked(wide, 2),
            stacked(d, 2),
            stacked(d, 2),
            pl.BlockSpec((rows, d), whole),
            pl.BlockSpec((8, cw), whole),
        ],
        scratch_shapes=[
            pltpu.VMEM((rows, wide), F32),
            pltpu.VMEM((rows, cw), F32),
            pltpu.VMEM((rows, di), F32),
            pltpu.VMEM((rows, di), F32),
            pltpu.VMEM((rows, d), F32),
            pltpu.VMEM((2, rows, LANE), F32),
            pltpu.VMEM((pairs, 8, rows), F32),
            pltpu.VMEM((rows, LANE), F32),
            pltpu.VMEM((pairs, 8, rows), F32),
            pltpu.VMEM((rows, LANE), F32),
            pltpu.VMEM((rows, rows), F32),
            pltpu.VMEM((rows, rows), F32),
            pltpu.VMEM((rows, rows), F32),
            pltpu.VMEM((2, rows, LANE), F32),
            pltpu.SemaphoreType.DMA((4,)),
        ],
    )
    outs = pl.pallas_call(
        bwd_kernel,
        grid_spec=grid_spec,
        out_shape=list(stacks)
        + [jax.ShapeDtypeStruct((rows, d), BF16), jax.ShapeDtypeStruct((8, cw), F32)],
        input_output_aliases={11 + k: k for k in range(len(held))},
        compiler_params=pltpu.CompilerParams(vmem_limit_bytes=VMEM_LIMIT),
        cost_estimate=pl.CostEstimate(
            flops=2 * rows * d * (wide + di), bytes_accessed=60 << 20, transcendentals=4 << 20
        ),
        name="mixer_backward",
    )(scal, cot, recv, resid, w_in, w_out_t, par, hp, *kept, *held)
    return outs[:3], outs[3], outs[4]


def ring_place(index, n):
    chip, core = index // 2, index % 2
    z, x = chip // 2, chip % 2
    return 2 * ((1 - x) * z + x * (n // 2 - 1 - z)) + core


def ring_device(place, n):
    spot, core = place // 2, place % 2
    far = spot // (n // 4)
    chip = (1 - far) * (2 * spot) + far * (2 * (n // 2 - 1 - spot) + 1)
    return 2 * chip + core


def tile_chunks(columns, parts):
    tiles = columns // LANE
    cuts = [LANE * (-(-tiles * i // parts)) for i in range(parts + 1)]
    return [(cuts[i], cuts[i + 1] - cuts[i]) for i in range(parts)]


def greet_all(n, me, section):
    barrier = pltpu.get_barrier_semaphore()

    def signal(i, carry):
        pl.semaphore_signal(
            barrier, inc=1, device_id=(section, (me + i) % n), device_id_type=pl.DeviceIdType.MESH
        )
        return carry

    lax.fori_loop(1, n, signal, 0)
    pl.semaphore_wait(barrier, n - 1)


def scatter_kernel(
    n, nin_t, gbr_t, gproj_hbm, nout_hbm, small_ref,
    gin_ref, gout_ref, small_out,
    gproj, nout, held, small_got, load_sem, send_sem, recv_sem, small_send, small_recv,
):
    me = lax.axis_index("dp")
    section = lax.axis_index("section")
    place = ring_place(me, n)
    steps = n // 2
    micros, rows = gproj_hbm.shape[0] - 1, gproj_hbm.shape[1]
    wide, di = gproj.shape[1], nout.shape[1]
    targets = (ring_device((place + 1) % n, n), ring_device((place + n - 1) % n, n))
    loads = []
    for m in range(micros):
        part = pl.ds(m * rows, rows)
        loads.append(pltpu.make_async_copy(nout_hbm.at[m], nout.at[part], load_sem.at[0, m]))
        loads.append(pltpu.make_async_copy(gproj_hbm.at[m], gproj.at[part], load_sem.at[1, m]))
    for load in loads:
        load.start()
    greet_all(n, me, section)

    def small_copy(other, slot):
        return pltpu.make_async_remote_copy(
            src_ref=small_ref.at[other],
            dst_ref=small_got.at[slot],
            send_sem=small_send.at[slot],
            recv_sem=small_recv.at[slot],
            device_id=(section, other),
            device_id_type=pl.DeviceIdType.MESH,
        )

    def small_start(i, carry):
        small_copy((me + i) % n, i).start()
        return carry

    lax.fori_loop(1, n, small_start, 0)
    for load in loads:
        load.wait()

    out_cuts = tile_chunks(di, 2)
    in_cuts = tile_chunks(wide, 4)
    chunks = [
        (False, *out_cuts[0]), (False, *out_cuts[1]),
        (True, *in_cuts[0]), (True, *in_cuts[2]), (True, *in_cuts[1]), (True, *in_cuts[3]),
    ]

    def own(owner, chunk):
        is_in, start, size = chunk
        if is_in:
            return dot_nn(nin_t[owner], gproj[:, start : start + size])
        return dot_nn(gbr_t[owner], nout[:, start : start + size])

    def columns(chunk):
        is_in, start, size = chunk
        return pl.ds(start if is_in else wide + start, size)

    def owner_of(way, k):
        shift = steps - k if way == 0 else n - steps + k
        return ring_device((place + shift) % n, n)

    def send(way, k, c):
        cols = columns(chunks[c])
        return pltpu.make_async_remote_copy(
            src_ref=held.at[way, k, :, cols],
            dst_ref=held.at[way, k + 1, :, cols],
            send_sem=send_sem.at[way, k, c],
            recv_sem=recv_sem.at[way, k, c],
            device_id=(section, targets[way]),
            device_id_type=pl.DeviceIdType.MESH,
        )

    def run_step(k, first, second):
        for c, chunk in enumerate(chunks):
            for way in range(2):
                if first and c % 2 != way:
                    continue
                cols = columns(chunk)
                total = own(owner_of(way, k), chunk)
                if not first and not (second and c % 2 != way):
                    send(way, k - 1, c).wait_recv()
                    total += held[way, k, :, cols].astype(F32)
                held[way, k, :, cols] = total.astype(BF16)
                send(way, k, c).start()

    run_step(0, True, False)
    run_step(1, False, True)

    def loop(k, carry):
        run_step(k, False, False)
        return carry

    lax.fori_loop(2, steps, loop, 0)

    for c, chunk in enumerate(chunks):
        is_in, start, size = chunk
        cols = columns(chunk)
        total = own(me, chunk)
        for way in range(2):
            send(way, steps - 1, c).wait_recv()
            total += held[way, steps, :, cols].astype(F32)
        if is_in:
            gin_ref[:, start : start + size] = total
        else:
            gout_ref[:, start : start + size] = total

    small_out[...] = small_ref[me]

    def small_end(i, carry):
        copy = small_copy((me + i) % n, i)
        copy.wait()
        small_out[...] += small_got[i]
        return carry

    lax.fori_loop(1, n, small_end, 0)
    for c in range(len(chunks)):
        send(c % 2, 0, c).wait_send()

    def sent(k, carry):
        for c in range(len(chunks)):
            for way in range(2):
                send(way, k, c).wait_send()
        return carry

    lax.fori_loop(1, steps, sent, 0)


def scatter_gradients(n, nin_t, gbr_t, gproj, nout, small):
    piece, tokens = nin_t.shape[1:]
    wide, di = gproj.shape[2], nout.shape[2]
    micros = nout.shape[0] - 1
    steps = n // 2
    vmem = pl.BlockSpec(memory_space=pltpu.VMEM)
    hbm = pl.BlockSpec(memory_space=pl.ANY)
    return pl.pallas_call(
        functools.partial(scatter_kernel, n),
        out_shape=[
            jax.ShapeDtypeStruct((piece, wide), F32),
            jax.ShapeDtypeStruct((piece, di), F32),
            jax.ShapeDtypeStruct(small.shape[1:], F32),
        ],
        in_specs=[vmem, vmem, hbm, hbm, vmem],
        out_specs=[vmem, vmem, vmem],
        scratch_shapes=[
            pltpu.VMEM((tokens, wide), BF16),
            pltpu.VMEM((tokens, di), BF16),
            pltpu.VMEM((2, steps + 1, piece, wide + di), BF16),
            pltpu.VMEM(small.shape, F32),
            pltpu.SemaphoreType.DMA((2, micros)),
            pltpu.SemaphoreType.DMA((2, steps, 6)),
            pltpu.SemaphoreType.DMA((2, steps, 6)),
            pltpu.SemaphoreType.DMA((n,)),
            pltpu.SemaphoreType.DMA((n,)),
        ],
        compiler_params=pltpu.CompilerParams(
            collective_id=0, has_side_effects=True, vmem_limit_bytes=VMEM_LIMIT
        ),
        cost_estimate=pl.CostEstimate(
            flops=2 * n * piece * tokens * (wide + di), bytes_accessed=20 << 20, transcendentals=0
        ),
        name="gradient_scatter",
    )(nin_t, gbr_t, gproj, nout, small)


def passed_along(shard, axis, by):
    length = lax.axis_size(axis)
    pairs = [(i, i + by) for i in range(length) if 0 <= i + by < length]
    return lax.ppermute(shard, axis, pairs)


def shards(
    x_in, lengths, norm_pre, w_in, conv_w, conv_b, dt_bias, a_log, skip_scale, norm_gate, w_out, cotangent
):
    section = lax.axis_index("section")
    micros, rows, d = x_in.shape
    heads = dt_bias.shape[1]
    taps = conv_w.shape[1]
    devices = lax.axis_size("dp")
    piece, wide = w_in.shape[1], w_in.shape[2]
    di = w_out.shape[1]
    cw_piece, gate_piece = conv_w.shape[2], norm_gate.shape[1]
    cw = cw_piece * devices
    pad = LANE - heads

    small = jnp.concatenate(
        [norm_pre[0], conv_b[0], norm_gate[0], conv_w[0].reshape(-1)]
    )
    small = jnp.pad(small, (0, piece * pad - small.shape[0])).reshape(piece, pad)
    gathered_in = lax.all_gather(jnp.concatenate([w_in[0], small], axis=1), "dp", axis=0, tiled=True)
    gathered_out = lax.all_gather(w_out[0].T, "dp", axis=0, tiled=True)
    tails = gathered_in[:, wide:].reshape(devices, piece * pad).astype(F32)
    ends = [0]
    for size in (piece, cw_piece, gate_piece, taps * cw_piece):
        ends.append(ends[-1] + size)
    gain_pre = tails[:, ends[0] : ends[1]].reshape(-1)
    conv_bias = tails[:, ends[1] : ends[2]].reshape(-1)
    gate_gain = tails[:, ends[2] : ends[3]].reshape(-1)
    conv_taps = tails[:, ends[3] : ends[4]].reshape(devices, taps, cw_piece)
    conv_taps = conv_taps.transpose(1, 0, 2).reshape(taps, cw)

    def wide_row(v):
        return jnp.pad(v, (0, cw - v.shape[0]))[None]

    par = jnp.concatenate(
        [
            conv_taps,
            conv_bias[None],
            wide_row(gate_gain),
            wide_row(jnp.repeat(skip_scale[0], di // heads)),
            wide_row(gain_pre),
        ],
        axis=0,
    )
    hp = jnp.pad(jnp.stack([dt_bias[0], -jnp.exp(a_log[0])]), ((0, 6), (0, pad)))

    first_end = lengths[:, 0, 0]
    second_end = first_end + lengths[:, 0, 1]
    slots = micros + 1

    def stack(width, dtype):
        return jax.ShapeDtypeStruct((slots, rows, width), dtype)

    stacks = (
        stack(d, BF16), stack(di, BF16), stack(d, F32), stack(d, F32),
        stack(wide + pad, F32), stack(cw, F32), stack(di, F32),
    )
    held = ()
    recv = jnp.zeros((rows, d), BF16)
    stats = jnp.zeros((8, LANE), F32)
    valid_total = jnp.zeros((), F32)
    for step_no in range(micros + 1):
        micro = step_no - section
        live = (micro >= 0) & (micro < micros)
        clipped = jnp.clip(micro, 0, micros - 1)
        scal = jnp.stack(
            [clipped, jnp.where(live, clipped, micros), first_end[clipped], second_end[clipped]]
        ).astype(jnp.int32)
        held, branch, stat = forward_step(scal, x_in, recv, gathered_in, gathered_out, par, hp, stacks, held)
        stats = stats + jnp.where(live, stat, 0.0)
        valid_total = valid_total + jnp.where(live, second_end[clipped], 0).astype(F32)
        if step_no < micros:
            recv = passed_along(branch, "section", 1)
    normed_in, normed_out, outputs, resid, proj, csum, mixed = held

    stacks = (stack(wide + pad, BF16), stack(d, BF16), stack(d, F32))
    back = ()
    recv = jnp.zeros((rows, d), BF16)
    packs = None
    for step_no in range(micros + 1):
        micro = step_no - 1 + section
        live = (micro >= 0) & (micro < micros)
        clipped = jnp.clip(micro, 0, micros - 1)
        scal = jnp.stack(
            [
                clipped, clipped, jnp.where(live, clipped, micros),
                first_end[clipped], second_end[clipped], live & (section == 1),
            ]
        ).astype(jnp.int32)
        back, sent, pack = backward_step(
            scal, cotangent, recv, gathered_in, gathered_out, par, hp, resid, (proj, csum, mixed), stacks, back
        )
        packs = pack if packs is None else packs + pack
        if step_no < micros:
            recv = passed_along(sent, "section", -1)
    grad_proj, grad_branch, in_grad = back

    def turned(v):
        return v[:micros].reshape(micros * rows, d).T.reshape(devices, piece, micros * rows)

    me = lax.axis_index("dp")
    per_head = packs[6, :di].reshape(heads, di // heads).sum(axis=1)
    common = jnp.concatenate(
        [
            packs[7, d : d + heads],
            packs[7, d + LANE : d + LANE + heads],
            per_head,
            stats[0, :2],
            valid_total[None],
        ]
    )
    small = jnp.concatenate(
        [
            packs[:taps].reshape(taps, devices, cw_piece).transpose(1, 0, 2).reshape(devices, -1),
            packs[4].reshape(devices, cw_piece),
            packs[5, :di].reshape(devices, gate_piece),
            packs[7, :d].reshape(devices, piece),
            jnp.broadcast_to(common, (devices, common.shape[0])),
        ],
        axis=1,
    )
    small_rows = -(-small.shape[1] // (8 * LANE)) * 8
    small = jnp.pad(small, ((0, 0), (0, small_rows * LANE - small.shape[1])))
    in_shard, out_shard, small = scatter_gradients(
        devices, turned(normed_in), turned(grad_branch), grad_proj, normed_out,
        small.reshape(devices, small_rows, LANE),
    )
    small = small.reshape(-1)
    parts = []
    start = 0
    for size in (taps * cw_piece, cw_piece, gate_piece, piece, heads, heads, heads, 3):
        parts.append(small[start : start + size])
        start += size
    sums = parts[7]
    rms = jnp.sqrt(sums[:2] / (sums[2] * d))

    return (
        outputs[:micros][None],
        in_grad[:micros][None],
        parts[3][None],
        in_shard[None, :, :wide],
        parts[0].reshape(1, taps, cw_piece),
        parts[1][None],
        parts[4][None],
        parts[5][None],
        parts[6][None],
        parts[2][None],
        out_shard.T[None],
        rms[None],
    )


def solution(mesh):
    placed = (
        P(None, "dp", None),
        P(None, "dp", None),
        P("section", "dp"),
        P("section", "dp", None),
        P("section", None, "dp"),
        P("section", "dp"),
        P("section", None),
        P("section", None),
        P("section", None),
        P("section", "dp"),
        P("section", None, "dp"),
        P(None, "dp", None),
    )
    return jax.shard_map(
        shards,
        mesh=mesh,
        in_specs=placed,
        out_specs=(
            P("section", None, "dp", None),
            P("section", None, "dp", None),
            P("section", "dp"),
            P("section", "dp", None),
            P("section", None, "dp"),
            P("section", "dp"),
            P("section", None),
            P("section", None),
            P("section", None),
            P("section", "dp"),
            P("section", None, "dp"),
            P("section", None),
        ),
        check_vma=False,
    )
```

```python
import functools

import jax
import jax.numpy as jnp
from jax import lax
from jax.experimental import pallas as pl
from jax.experimental.pallas import tpu as pltpu
from jax.sharding import PartitionSpec as P

EPS = 1e-05
F32 = jnp.float32
BF16 = jnp.bfloat16
LANE = 128
LOG2E = 1.4426950408889634
NEG = -1e30
VMEM_LIMIT = 60 * 1024 * 1024
HIGH = lax.Precision.HIGHEST
MIXER_VMEM = 63 * 1024 * 1024
IN_TILE = 384
OUT_TILE = 256


def dot_nn(a, b, precision=None):
    return lax.dot_general(
        a, b, (((1,), (0,)), ((), ())), preferred_element_type=F32, precision=precision
    )


def dot_nt(a, b, precision=None):
    return lax.dot_general(
        a, b, (((1,), (1,)), ((), ())), preferred_element_type=F32, precision=precision
    )


def dot_tn(a, b, precision=None):
    return lax.dot_general(
        a, b, (((0,), (0,)), ((), ())), preferred_element_type=F32, precision=precision
    )


def sigmoid(v):
    return 1.0 / (1.0 + jnp.exp(-v))


def iota(shape, dim):
    return lax.broadcasted_iota(jnp.int32, shape, dim)


def row_sum(v):
    return jnp.sum(v, axis=1, keepdims=True)


def col_sum(v):
    return jnp.sum(v, axis=0, keepdims=True)


def segments_of(position, first_end, second_end):
    return (position >= first_end).astype(jnp.int32) + (position >= second_end).astype(jnp.int32)


def decay_terms(dt_raw, hp_ref, rows):
    z = dt_raw + hp_ref[0:1, :]
    step = jnp.maximum(z, 0.0) + jnp.log1p(jnp.exp(-jnp.abs(z)))
    below = (iota((rows, rows), 1) <= iota((rows, rows), 0)).astype(F32)
    ld = dot_nn(below, step * (hp_ref[1:2, :] * LOG2E), HIGH)
    lr = ld - jnp.log2(jnp.maximum(step, 1e-37))
    return z, step, ld, lr


def to_rows(v, out_ref, pairs):
    vt = v.T
    for p in range(pairs):
        out_ref[p, 0:2, :] = vt[2 * p : 2 * p + 2, :]


def pair_lanes(ref, p):
    return pltpu.roll(ref[...], lax.rem(LANE - 2 * p, LANE), 1)


def mixer_kernel(
    ends, x_hbm, cot_hbm, win_hbm, wout_hbm, par_ref, hp_ref,
    out_hbm, ing_hbm, nin_hbm, nout_hbm, gproj_hbm, gbr_hbm, proj_hbm, csum_hbm, mixed_hbm,
    pack_ref, stat_ref,
    win, wout, xs, cot, recv, sent, nin, nout, gbr, gproj, proj, csum, mixed, wide_s, stage,
    act_bc, cols_s, rows_s, row_q, col_q, cb, dcb, maskb, stat,
    load_sem, weight_sem, save_sem, store_sem, send_sem, recv_sem,
):
    section = lax.axis_index("section")
    me = lax.axis_index("dp")
    micros = x_hbm.shape[0]
    rows, d = nin.shape
    di, cw = mixed.shape[1], csum.shape[1]
    half = rows // 2
    pairs = di // LANE
    wide = proj.shape[1]
    lane = iota((rows, LANE), 1)
    first = lane < LANE // 2
    pos = iota((rows, LANE), 0)
    x_loads = [pltpu.make_async_copy(x_hbm.at[m], xs.at[m], load_sem.at[m]) for m in range(micros)]
    cot_loads = [
        pltpu.make_async_copy(cot_hbm.at[m], cot.at[m], load_sem.at[micros + m]) for m in range(micros)
    ]

    def tile(j, size):
        return pl.ds(pl.multiple_of(j * size, size), size)

    def weight_load(c):
        return pltpu.make_async_copy(
            win_hbm.at[:, tile(c, IN_TILE)], win.at[:, tile(c, IN_TILE)], weight_sem.at[c]
        )

    out_load = pltpu.make_async_copy(wout_hbm, wout, weight_sem.at[wide // IN_TILE])
    saves = [
        pltpu.make_async_copy(v, to, save_sem.at[i])
        for i, (v, to) in enumerate(((proj, proj_hbm), (csum, csum_hbm), (mixed, mixed_hbm)))
    ]
    restores = [
        pltpu.make_async_copy(to, v, save_sem.at[i])
        for i, (v, to) in enumerate(((proj, proj_hbm), (csum, csum_hbm), (mixed, mixed_hbm)))
    ]

    results = (
        (nin, nin_hbm), (nout, nout_hbm), (stage, out_hbm),
        (gbr, gbr_hbm), (gproj, gproj_hbm), (stage, ing_hbm),
    )

    def store(m, i):
        return pltpu.make_async_copy(results[i][0], results[i][1].at[m], store_sem.at[i])

    def hand_over(m, j):
        part = tile(j, OUT_TILE)
        return pltpu.make_async_remote_copy(
            src_ref=sent.at[m, :, part],
            dst_ref=recv.at[m, :, part],
            send_sem=send_sem.at[m, j],
            recv_sem=recv_sem.at[m, j],
            device_id=(1 - section, me),
            device_id_type=pl.DeviceIdType.MESH,
        )

    hands = d // OUT_TILE

    def repeat(count, body):
        def step(i, carry):
            body(i)
            return carry

        lax.fori_loop(0, count, step, 0)

    for copy in x_loads + cot_loads:
        copy.start()
    repeat(wide // IN_TILE, lambda c: weight_load(c).start())
    out_load.start()
    recv[...] = jnp.zeros_like(recv)
    pack_ref[...] = jnp.zeros_like(pack_ref)
    stat_ref[...] = jnp.zeros_like(stat_ref)
    barrier = pltpu.get_barrier_semaphore()
    pl.semaphore_signal(barrier, inc=1, device_id=(1 - section, me), device_id_type=pl.DeviceIdType.MESH)
    pl.semaphore_wait(barrier, 1)

    def input_of(m, cols):
        u = xs[m, :, cols].astype(F32)
        return u + jnp.where(section == 1, recv[m, :, cols].astype(F32), 0.0)

    def set_mask(e1, e2, upper):
        rpos, cpos = iota((rows, rows), 0), iota((rows, rows), 1)
        keep = (rpos <= cpos) if upper else (rpos >= cpos)
        keep &= segments_of(rpos, e1, e2) == segments_of(cpos, e1, e2)
        maskb[...] = jnp.where(keep, 0.0, NEG)

    def forward(m):
        e1, e2 = ends[m, 0], ends[m, 1]
        x_loads[m].wait()

        @pl.when(section == 1)
        def _():
            repeat(hands, lambda j: hand_over(m, j).wait_recv())

        u = input_of(m, slice(None))
        q = lax.rsqrt(jnp.mean(u * u, axis=1, keepdims=True) + EPS)
        if m > 0:
            for copy in [store(m - 1, i) for i in range(3)] + saves:
                copy.wait()
        nin[...] = (u * q * par_ref[7:8, :d]).astype(BF16)
        store(m, 0).start()

        def project(c):
            if m == 0:
                weight_load(c).wait()
            proj[:, tile(c, IN_TILE)] = dot_nn(nin[...], win[:, tile(c, IN_TILE)])

        repeat(wide // IN_TILE, project)
        if m < micros - 1:
            saves[0].start()
        dist = pos - jnp.where(pos >= e2, e2, jnp.where(pos >= e1, e1, 0))

        def conv_tile(j):
            here = tile(j, LANE)
            v = proj[:, pl.ds(pl.multiple_of(di + j * LANE, LANE), LANE)]
            acc = par_ref[4:5, here] + par_ref[3:4, here] * v
            for lag in range(1, 4):
                acc += par_ref[3 - lag : 4 - lag, here] * jnp.where(
                    dist >= lag, pltpu.roll(v, lag, 0), 0.0
                )
            csum[:, here] = acc

        repeat(cw // LANE, conv_tile)
        if m < micros - 1:
            saves[1].start()
        _, _, ld, lr = decay_terms(proj[:, di + cw :], hp_ref, rows)
        cols_s[...] = ld
        to_rows(lr, rows_s, pairs)
        for j in range(2):
            v = csum[:, di + j * LANE : di + (j + 1) * LANE]
            act_bc[j] = v * sigmoid(v)
        cb[...] = dot_nt(act_bc[1], act_bc[0], HIGH)
        set_mask(e1, e2, False)

        def pair(p, sq):
            here = tile(p, LANE)
            cs = csum[:, here]
            x = cs * sigmoid(cs)
            ldr = pair_lanes(cols_s, p)
            y0 = jnp.zeros((half, LANE), F32)
            y1 = jnp.zeros((half, LANE), F32)
            for h in range(2):
                xm = jnp.where(first if h == 0 else ~first, x, 0.0).astype(BF16)
                lc = ldr[:, h : h + 1]
                lrow = rows_s[p, h : h + 1, :]
                m0 = jnp.exp2((lc[:half] - lrow[:, :half]) + maskb[:half, :half]) * cb[:half, :half]
                m1 = jnp.exp2((lc[half:] - lrow) + maskb[half:, :]) * cb[half:, :]
                y0 += dot_nn(m0.astype(BF16), xm[:half])
                y1 += dot_nn(m1.astype(BF16), xm)
            y = jnp.concatenate([y0, y1], axis=0) + par_ref[6:7, here] * x
            mixed[:, here] = y
            gate = proj[:, here]
            g = y * (gate * sigmoid(gate))
            wide_s[:, here] = g
            return sq + g * g

        sq = lax.fori_loop(0, pairs, pair, jnp.zeros((rows, LANE), F32))
        if m < micros - 1:
            saves[2].start()
        r = lax.rsqrt(row_sum(sq) * (1.0 / di) + EPS)
        nout[...] = (wide_s[...] * r * par_ref[5:6, :di]).astype(BF16)
        store(m, 1).start()
        if m == 0:
            out_load.wait()
        valid = iota((rows, 1), 0) < e2

        def branch_tile(j):
            here = tile(j, OUT_TILE)
            branch = dot_nt(nout[...], wout[here, :])
            u = input_of(m, here)
            stage[:, here] = u + branch

            @pl.when(section == 0)
            def _():
                sent[m, :, here] = branch.astype(BF16)
                hand_over(m, j).start()

            usq = col_sum(row_sum(jnp.where(valid, u * u, 0.0)))
            bsq = col_sum(row_sum(jnp.where(valid, branch * branch, 0.0)))
            at = iota((8, LANE), 1)
            stat_ref[...] += jnp.where(at == 0, usq, jnp.where(at == 1, bsq, 0.0))

        repeat(hands, branch_tile)
        store(m, 2).start()

    def backward(m):
        e1, e2 = ends[m, 0], ends[m, 1]
        newest = m == micros - 1

        @pl.when(section == 0)
        def _():
            repeat(hands, lambda j: hand_over(m, j).wait_recv())

        cot_loads[m].wait()
        valid = (iota((rows, 1), 0) < e2).astype(F32)
        if not newest:
            store(m + 1, 3).wait()
        gbr[...] = jnp.where(
            section == 1, cot[m].astype(F32) * valid, recv[m].astype(F32)
        ).astype(BF16)
        store(m, 3).start()
        if not newest:
            for copy in restores:
                copy.wait()

        def gate_tile(c, carry):
            gn = dot_nn(gbr[...], wout[:, tile(c, IN_TILE)])
            wide_s[:, tile(c, IN_TILE)] = gn
            sq, cross = carry
            for j in range(IN_TILE // LANE):
                here = pl.ds(pl.multiple_of(c * IN_TILE + j * LANE, LANE), LANE)
                gate = proj[:, here]
                gated = mixed[:, here] * (gate * sigmoid(gate))
                sq += gated * gated
                cross += gated * (par_ref[5:6, here] * gn[:, j * LANE : (j + 1) * LANE])
            return sq, cross

        zero = jnp.zeros((rows, LANE), F32)
        sq, cross = lax.fori_loop(0, di // IN_TILE, gate_tile, (zero, zero))
        r = lax.rsqrt(row_sum(sq) * (1.0 / di) + EPS)
        rc = r * r * r * (row_sum(cross) * (1.0 / di))
        stat[0] = jnp.broadcast_to(r, (rows, LANE))
        stat[1] = jnp.broadcast_to(rc, (rows, LANE))
        z, dt, ld, lr = decay_terms(proj[:, di + cw :], hp_ref, rows)
        cols_s[...] = lr
        to_rows(ld, rows_s, pairs)
        for j in range(2):
            v = csum[:, di + j * LANE : di + (j + 1) * LANE]
            act_bc[j] = v * sigmoid(v)
        cb[...] = dot_nt(act_bc[0], act_bc[1], HIGH)
        set_mask(e1, e2, True)
        dcb[...] = jnp.zeros_like(dcb)
        col_q[...] = jnp.zeros_like(col_q)
        ahead = jnp.where(pos < e1, e1, jnp.where(pos < e2, e2, rows)) - pos
        if not newest:
            store(m + 1, 4).wait()

        def conv_back(dcv, off):
            here = pl.ds(off, LANE)
            there = pl.ds(pl.multiple_of(di + off, LANE), LANE)
            v = proj[:, there]
            out = par_ref[3:4, here] * dcv
            pack_ref[3:4, here] += col_sum(dcv * v)
            pack_ref[4:5, here] += col_sum(dcv)
            for lag in range(1, 4):
                moved = jnp.where(ahead > lag, pltpu.roll(dcv, rows - lag, 0), 0.0)
                out += par_ref[3 - lag : 4 - lag, here] * moved
                pack_ref[3 - lag : 4 - lag, here] += col_sum(moved * v)
            gproj[:, there] = out.astype(BF16)

        def pair(p):
            off = pl.multiple_of(p * LANE, LANE)
            here = pl.ds(off, LANE)
            gate = proj[:, here]
            mx = mixed[:, here]
            gnt = wide_s[:, here]
            sg = sigmoid(gate)
            sil = gate * sg
            gated = mx * sil
            pack_ref[5:6, here] += col_sum(gated * stat[0] * gnt)
            gg = stat[0] * (par_ref[5:6, here] * gnt) - gated * stat[1]
            dy = gg * sil
            gproj[:, here] = (gg * mx * (sg * (1.0 + gate * (1.0 - sg)))).astype(BF16)
            cs = csum[:, here]
            sc = sigmoid(cs)
            x = cs * sc
            pack_ref[6:7, here] += col_sum(dy * x)
            xb = x.astype(BF16)
            lrr = pair_lanes(cols_s, p)
            dx0 = jnp.zeros((half, LANE), F32)
            dx1 = jnp.zeros((half, LANE), F32)
            for h in range(2):
                dym = jnp.where(first if h == 0 else ~first, dy, 0.0).astype(BF16)
                lc = lrr[:, h : h + 1]
                lrow = rows_s[p, h : h + 1, :]
                d0 = jnp.exp2((lrow - lc[:half]) + maskb[:half, :])
                d1 = jnp.exp2((lrow[:, half:] - lc[half:]) + maskb[half:, half:])
                t0 = dot_nt(xb[:half], dym) * d0
                t1 = dot_nt(xb[half:], dym[half:]) * d1
                dx0 += dot_nn((d0 * cb[:half, :]).astype(BF16), dym)
                dx1 += dot_nn((d1 * cb[half:, half:]).astype(BF16), dym[half:])
                dcb[:half, :] += t0
                dcb[half:, half:] += t1
                q0 = t0 * cb[:half, :]
                q1 = t1 * cb[half:, half:]
                row_q[p, h : h + 1, :half] = col_sum(q0[:, :half])
                row_q[p, h : h + 1, half:] = col_sum(q0[:, half:]) + col_sum(q1)
                picked = lane == 2 * p + h
                col_q[:half, :] = jnp.where(picked[:half], row_sum(q0), col_q[:half, :])
                col_q[half:, :] = jnp.where(picked[half:], row_sum(q1), col_q[half:, :])
            dx = jnp.concatenate([dx0, dx1], axis=0) + par_ref[6:7, here] * dy
            conv_back(dx * (sc * (1.0 + cs * (1.0 - sc))), off)

        repeat(pairs, pair)
        total = dcb[...]
        for j, grad in enumerate((dot_nn(total, act_bc[1], HIGH), dot_tn(total, act_bc[0], HIGH))):
            cs = csum[:, di + j * LANE : di + (j + 1) * LANE]
            sc = sigmoid(cs)
            conv_back(grad * (sc * (1.0 + cs * (1.0 - sc))), di + j * LANE)
        spread = jnp.concatenate(
            [row_q[p, 0:2, :] for p in range(pairs)]
            + [jnp.zeros((LANE - 2 * pairs, rows), F32)],
            axis=0,
        )
        colq = col_q[...]
        above = (iota((rows, rows), 1) >= iota((rows, rows), 0)).astype(F32)
        after = dot_nn(above, spread.T - colq, HIGH)
        sz = sigmoid(z)
        ratio = jnp.where(z < -20.0, 1.0, sz / jnp.maximum(dt, 1e-37))
        neg_rate = hp_ref[1:2, :]
        ddt = jnp.where(lane < 2 * pairs, colq * ratio + neg_rate * after * sz, 0.0)
        gproj[:, di + cw :] = ddt.astype(BF16)
        pack_ref[7:8, d : d + LANE] += col_sum(ddt)
        pack_ref[7:8, d + LANE : d + 2 * LANE] += col_sum(
            jnp.where(lane < 2 * pairs, neg_rate * dt * after, 0.0)
        )
        store(m, 4).start()
        if m > 0:
            for copy in restores:
                copy.start()
        if newest:
            store(m, 2).wait()
        else:
            store(m + 1, 5).wait()

        def back_tile(j):
            stage[:, tile(j, OUT_TILE)] = dot_nt(gproj[...], win[tile(j, OUT_TILE), :])

        repeat(hands, back_tile)
        u = input_of(m, slice(None))
        q = lax.rsqrt(jnp.mean(u * u, axis=1, keepdims=True) + EPS)
        gi = stage[...]
        uq3 = q * q * q * jnp.mean(u * (par_ref[7:8, :d] * gi), axis=1, keepdims=True)
        pack_ref[7:8, :d] += col_sum(u * q * gi)

        def end_tile(j):
            here = tile(j, OUT_TILE)
            grad = (
                gbr[:, here].astype(F32)
                + q * (par_ref[7:8, here] * stage[:, here])
                - input_of(m, here) * uq3
            )
            stage[:, here] = grad

            @pl.when(section == 1)
            def _():
                sent[m, :, here] = grad.astype(BF16)
                hand_over(m, j).start()

        repeat(hands, end_tile)
        store(m, 5).start()

    for m in range(micros):
        forward(m)
    for i in range(2):
        store(micros - 1, i).wait()
    for m in reversed(range(micros)):
        backward(m)
    for i in range(3, 6):
        store(0, i).wait()
    for m in range(micros):
        repeat(hands, lambda j: hand_over(m, j).wait_send())


def mixer_steps(ends, x_in, cot, w_in, w_out_t, par, hp):
    micros, rows, d = x_in.shape
    di = w_out_t.shape[1]
    wide = w_in.shape[1]
    cw = par.shape[1]
    pairs = di // LANE
    hands = d // OUT_TILE
    hbm = pl.BlockSpec(memory_space=pl.ANY)
    vmem = pl.BlockSpec(memory_space=pltpu.VMEM)

    def stack(width, dtype):
        return jax.ShapeDtypeStruct((micros, rows, width), dtype)

    return pl.pallas_call(
        mixer_kernel,
        in_specs=[pl.BlockSpec(memory_space=pltpu.SMEM)] + [hbm] * 4 + [vmem] * 2,
        out_specs=[hbm] * 9 + [vmem] * 2,
        out_shape=[
            stack(d, F32), stack(d, F32), stack(d, BF16), stack(di, BF16), stack(wide, BF16), stack(d, BF16),
            jax.ShapeDtypeStruct((rows, wide), F32),
            jax.ShapeDtypeStruct((rows, cw), F32),
            jax.ShapeDtypeStruct((rows, di), F32),
            jax.ShapeDtypeStruct((8, cw), F32),
            jax.ShapeDtypeStruct((8, LANE), F32),
        ],
        scratch_shapes=[
            pltpu.VMEM((d, wide), BF16),
            pltpu.VMEM((d, di), BF16),
            pltpu.VMEM((micros, rows, d), BF16),
            pltpu.VMEM((micros, rows, d), BF16),
            pltpu.VMEM((micros, rows, d), BF16),
            pltpu.VMEM((micros, rows, d), BF16),
            pltpu.VMEM((rows, d), BF16),
            pltpu.VMEM((rows, di), BF16),
            pltpu.VMEM((rows, d), BF16),
            pltpu.VMEM((rows, wide), BF16),
            pltpu.VMEM((rows, wide), F32),
            pltpu.VMEM((rows, cw), F32),
            pltpu.VMEM((rows, di), F32),
            pltpu.VMEM((rows, di), F32),
            pltpu.VMEM((rows, d), F32),
            pltpu.VMEM((2, rows, LANE), F32),
            pltpu.VMEM((rows, LANE), F32),
            pltpu.VMEM((pairs, 8, rows), F32),
            pltpu.VMEM((pairs, 8, rows), F32),
            pltpu.VMEM((rows, LANE), F32),
            pltpu.VMEM((rows, rows), F32),
            pltpu.VMEM((rows, rows), F32),
            pltpu.VMEM((rows, rows), F32),
            pltpu.VMEM((2, rows, LANE), F32),
            pltpu.SemaphoreType.DMA((2 * micros,)),
            pltpu.SemaphoreType.DMA((wide // IN_TILE + 1,)),
            pltpu.SemaphoreType.DMA((3,)),
            pltpu.SemaphoreType.DMA((6,)),
            pltpu.SemaphoreType.DMA((micros, hands)),
            pltpu.SemaphoreType.DMA((micros, hands)),
        ],
        compiler_params=pltpu.CompilerParams(
            collective_id=1, has_side_effects=True, vmem_limit_bytes=MIXER_VMEM
        ),
        cost_estimate=pl.CostEstimate(
            flops=12 * rows * d * (wide + di), bytes_accessed=100 << 20, transcendentals=16 << 20
        ),
        name="mixer_steps",
    )(ends, x_in, cot, w_in, w_out_t, par, hp)


def ring_place(index, n):
    chip, core = index // 2, index % 2
    z, x = chip // 2, chip % 2
    return 2 * ((1 - x) * z + x * (n // 2 - 1 - z)) + core


def ring_device(place, n):
    spot, core = place // 2, place % 2
    far = spot // (n // 4)
    chip = (1 - far) * (2 * spot) + far * (2 * (n // 2 - 1 - spot) + 1)
    return 2 * chip + core


def tile_chunks(columns, parts):
    tiles = columns // LANE
    cuts = [LANE * (-(-tiles * i // parts)) for i in range(parts + 1)]
    return [(cuts[i], cuts[i + 1] - cuts[i]) for i in range(parts)]


def greet_all(n, me, section):
    barrier = pltpu.get_barrier_semaphore()

    def signal(i, carry):
        pl.semaphore_signal(
            barrier, inc=1, device_id=(section, (me + i) % n), device_id_type=pl.DeviceIdType.MESH
        )
        return carry

    lax.fori_loop(1, n, signal, 0)
    pl.semaphore_wait(barrier, n - 1)


def scatter_kernel(
    n, nin_t, gbr_t, gproj_hbm, nout_hbm, small_ref,
    gin_ref, gout_ref, small_out,
    gproj, nout, held, small_got, load_sem, send_sem, recv_sem, small_send, small_recv,
):
    me = lax.axis_index("dp")
    section = lax.axis_index("section")
    place = ring_place(me, n)
    steps = n // 2
    micros, rows = gproj_hbm.shape[0], gproj_hbm.shape[1]
    wide, di = gproj.shape[1], nout.shape[1]
    targets = (ring_device((place + 1) % n, n), ring_device((place + n - 1) % n, n))
    loads = []
    for m in range(micros):
        part = pl.ds(m * rows, rows)
        loads.append(pltpu.make_async_copy(nout_hbm.at[m], nout.at[part], load_sem.at[0, m]))
        loads.append(pltpu.make_async_copy(gproj_hbm.at[m], gproj.at[part], load_sem.at[1, m]))
    for load in loads:
        load.start()
    greet_all(n, me, section)

    def small_copy(other, slot):
        return pltpu.make_async_remote_copy(
            src_ref=small_ref.at[other],
            dst_ref=small_got.at[slot],
            send_sem=small_send.at[slot],
            recv_sem=small_recv.at[slot],
            device_id=(section, other),
            device_id_type=pl.DeviceIdType.MESH,
        )

    def small_start(i, carry):
        small_copy((me + i) % n, i).start()
        return carry

    lax.fori_loop(1, n, small_start, 0)
    for load in loads:
        load.wait()

    out_cuts = tile_chunks(di, 2)
    in_cuts = tile_chunks(wide, 4)
    chunks = [
        (False, *out_cuts[0]), (False, *out_cuts[1]),
        (True, *in_cuts[0]), (True, *in_cuts[2]), (True, *in_cuts[1]), (True, *in_cuts[3]),
    ]

    def own(owner, chunk):
        is_in, start, size = chunk
        if is_in:
            return dot_nn(nin_t[owner], gproj[:, start : start + size])
        return dot_nn(gbr_t[owner], nout[:, start : start + size])

    def columns(chunk):
        is_in, start, size = chunk
        return pl.ds(start if is_in else wide + start, size)

    def owner_of(way, k):
        shift = steps - k if way == 0 else n - steps + k
        return ring_device((place + shift) % n, n)

    def send(way, k, c):
        cols = columns(chunks[c])
        return pltpu.make_async_remote_copy(
            src_ref=held.at[way, k, :, cols],
            dst_ref=held.at[way, k + 1, :, cols],
            send_sem=send_sem.at[way, k, c],
            recv_sem=recv_sem.at[way, k, c],
            device_id=(section, targets[way]),
            device_id_type=pl.DeviceIdType.MESH,
        )

    def run_step(k, first, second):
        for c, chunk in enumerate(chunks):
            for way in range(2):
                if first and c % 2 != way:
                    continue
                cols = columns(chunk)
                total = own(owner_of(way, k), chunk)
                if not first and not (second and c % 2 != way):
                    send(way, k - 1, c).wait_recv()
                    total += held[way, k, :, cols].astype(F32)
                held[way, k, :, cols] = total.astype(BF16)
                send(way, k, c).start()

    run_step(0, True, False)
    run_step(1, False, True)

    def loop(k, carry):
        run_step(k, False, False)
        return carry

    lax.fori_loop(2, steps, loop, 0)

    for c, chunk in enumerate(chunks):
        is_in, start, size = chunk
        cols = columns(chunk)
        total = own(me, chunk)
        for way in range(2):
            send(way, steps - 1, c).wait_recv()
            total += held[way, steps, :, cols].astype(F32)
        if is_in:
            gin_ref[:, start : start + size] = total
        else:
            gout_ref[:, start : start + size] = total

    small_out[...] = small_ref[me]

    def small_end(i, carry):
        copy = small_copy((me + i) % n, i)
        copy.wait()
        small_out[...] += small_got[i]
        return carry

    lax.fori_loop(1, n, small_end, 0)
    for c in range(len(chunks)):
        send(c % 2, 0, c).wait_send()

    def sent(k, carry):
        for c in range(len(chunks)):
            for way in range(2):
                send(way, k, c).wait_send()
        return carry

    lax.fori_loop(1, steps, sent, 0)


def scatter_gradients(n, nin_t, gbr_t, gproj, nout, small):
    piece, tokens = nin_t.shape[1:]
    wide, di = gproj.shape[2], nout.shape[2]
    micros = nout.shape[0]
    steps = n // 2
    vmem = pl.BlockSpec(memory_space=pltpu.VMEM)
    hbm = pl.BlockSpec(memory_space=pl.ANY)
    return pl.pallas_call(
        functools.partial(scatter_kernel, n),
        out_shape=[
            jax.ShapeDtypeStruct((piece, wide), F32),
            jax.ShapeDtypeStruct((piece, di), F32),
            jax.ShapeDtypeStruct(small.shape[1:], F32),
        ],
        in_specs=[vmem, vmem, hbm, hbm, vmem],
        out_specs=[vmem, vmem, vmem],
        scratch_shapes=[
            pltpu.VMEM((tokens, wide), BF16),
            pltpu.VMEM((tokens, di), BF16),
            pltpu.VMEM((2, steps + 1, piece, wide + di), BF16),
            pltpu.VMEM(small.shape, F32),
            pltpu.SemaphoreType.DMA((2, micros)),
            pltpu.SemaphoreType.DMA((2, steps, 6)),
            pltpu.SemaphoreType.DMA((2, steps, 6)),
            pltpu.SemaphoreType.DMA((n,)),
            pltpu.SemaphoreType.DMA((n,)),
        ],
        compiler_params=pltpu.CompilerParams(
            collective_id=0, has_side_effects=True, vmem_limit_bytes=VMEM_LIMIT
        ),
        cost_estimate=pl.CostEstimate(
            flops=2 * n * piece * tokens * (wide + di), bytes_accessed=20 << 20, transcendentals=0
        ),
        name="gradient_scatter",
    )(nin_t, gbr_t, gproj, nout, small)


def shards(
    x_in, lengths, norm_pre, w_in, conv_w, conv_b, dt_bias, a_log, skip_scale, norm_gate, w_out, cotangent
):
    micros, rows, d = x_in.shape
    heads = dt_bias.shape[1]
    taps = conv_w.shape[1]
    devices = lax.axis_size("dp")
    piece, wide = w_in.shape[1], w_in.shape[2]
    di = w_out.shape[1]
    cw_piece, gate_piece = conv_w.shape[2], norm_gate.shape[1]
    cw = cw_piece * devices
    pad = LANE - heads

    small = jnp.concatenate(
        [norm_pre[0], conv_b[0], norm_gate[0], conv_w[0].reshape(-1)]
    )
    small = jnp.pad(small, (0, piece * pad - small.shape[0])).reshape(piece, pad)
    gathered_in = lax.all_gather(jnp.concatenate([w_in[0], small], axis=1), "dp", axis=0, tiled=True)
    gathered_out = lax.all_gather(w_out[0].T, "dp", axis=0, tiled=True)
    tails = gathered_in[:, wide:].reshape(devices, piece * pad).astype(F32)
    ends = [0]
    for size in (piece, cw_piece, gate_piece, taps * cw_piece):
        ends.append(ends[-1] + size)
    gain_pre = tails[:, ends[0] : ends[1]].reshape(-1)
    conv_bias = tails[:, ends[1] : ends[2]].reshape(-1)
    gate_gain = tails[:, ends[2] : ends[3]].reshape(-1)
    conv_taps = tails[:, ends[3] : ends[4]].reshape(devices, taps, cw_piece)
    conv_taps = conv_taps.transpose(1, 0, 2).reshape(taps, cw)

    def wide_row(v):
        return jnp.pad(v, (0, cw - v.shape[0]))[None]

    par = jnp.concatenate(
        [
            conv_taps,
            conv_bias[None],
            wide_row(gate_gain),
            wide_row(jnp.repeat(skip_scale[0], di // heads)),
            wide_row(gain_pre),
        ],
        axis=0,
    )
    hp = jnp.pad(jnp.stack([dt_bias[0], -jnp.exp(a_log[0])]), ((0, 6), (0, pad)))

    first_end = lengths[:, 0, 0]
    second_end = first_end + lengths[:, 0, 1]
    ends = jnp.stack([first_end, second_end], axis=1)
    (outputs, in_grad, normed_in, normed_out, grad_proj, grad_branch, _, _, _, packs, stats) = mixer_steps(
        ends, x_in, cotangent, gathered_in, gathered_out, par, hp
    )
    valid_total = jnp.sum(second_end).astype(F32)

    def turned(v):
        return v.reshape(micros * rows, d).T.reshape(devices, piece, micros * rows)

    me = lax.axis_index("dp")
    per_head = packs[6, :di].reshape(heads, di // heads).sum(axis=1)
    common = jnp.concatenate(
        [
            packs[7, d : d + heads],
            packs[7, d + LANE : d + LANE + heads],
            per_head,
            stats[0, :2],
            valid_total[None],
        ]
    )
    small = jnp.concatenate(
        [
            packs[:taps].reshape(taps, devices, cw_piece).transpose(1, 0, 2).reshape(devices, -1),
            packs[4].reshape(devices, cw_piece),
            packs[5, :di].reshape(devices, gate_piece),
            packs[7, :d].reshape(devices, piece),
            jnp.broadcast_to(common, (devices, common.shape[0])),
        ],
        axis=1,
    )
    small_rows = -(-small.shape[1] // (8 * LANE)) * 8
    small = jnp.pad(small, ((0, 0), (0, small_rows * LANE - small.shape[1])))
    in_shard, out_shard, small = scatter_gradients(
        devices, turned(normed_in), turned(grad_branch), grad_proj, normed_out,
        small.reshape(devices, small_rows, LANE),
    )
    small = small.reshape(-1)
    parts = []
    start = 0
    for size in (taps * cw_piece, cw_piece, gate_piece, piece, heads, heads, heads, 3):
        parts.append(small[start : start + size])
        start += size
    sums = parts[7]
    rms = jnp.sqrt(sums[:2] / (sums[2] * d))

    return (
        outputs[None],
        in_grad[None],
        parts[3][None],
        in_shard[None, :, :wide],
        parts[0].reshape(1, taps, cw_piece),
        parts[1][None],
        parts[4][None],
        parts[5][None],
        parts[6][None],
        parts[2][None],
        out_shard.T[None],
        rms[None],
    )


def solution(mesh):
    placed = (
        P(None, "dp", None),
        P(None, "dp", None),
        P("section", "dp"),
        P("section", "dp", None),
        P("section", None, "dp"),
        P("section", "dp"),
        P("section", None),
        P("section", None),
        P("section", None),
        P("section", "dp"),
        P("section", None, "dp"),
        P(None, "dp", None),
    )
    return jax.shard_map(
        shards,
        mesh=mesh,
        in_specs=placed,
        out_specs=(
            P("section", None, "dp", None),
            P("section", None, "dp", None),
            P("section", "dp"),
            P("section", "dp", None),
            P("section", None, "dp"),
            P("section", "dp"),
            P("section", None),
            P("section", None),
            P("section", None),
            P("section", "dp"),
            P("section", None, "dp"),
            P("section", None),
        ),
        check_vma=False,
    )
```

```python
import functools

import jax
import jax.numpy as jnp
from jax import lax
from jax.experimental import pallas as pl
from jax.experimental.pallas import tpu as pltpu
from jax.sharding import PartitionSpec as P

EPS = 1e-05
F32 = jnp.float32
BF16 = jnp.bfloat16
LANE = 128
LOG2E = 1.4426950408889634
NEG = -1e30
VMEM_LIMIT = 60 * 1024 * 1024
HIGH = lax.Precision.HIGHEST
MIXER_VMEM = 63 * 1024 * 1024
IN_TILE = 384
OUT_TILE = 256


def dot_nn(a, b, precision=None):
    return lax.dot_general(
        a, b, (((1,), (0,)), ((), ())), preferred_element_type=F32, precision=precision
    )


def dot_nt(a, b, precision=None):
    return lax.dot_general(
        a, b, (((1,), (1,)), ((), ())), preferred_element_type=F32, precision=precision
    )


def dot_tn(a, b, precision=None):
    return lax.dot_general(
        a, b, (((0,), (0,)), ((), ())), preferred_element_type=F32, precision=precision
    )


def sigmoid(v):
    return 1.0 / (1.0 + jnp.exp(-v))


def iota(shape, dim):
    return lax.broadcasted_iota(jnp.int32, shape, dim)


def row_sum(v):
    return jnp.sum(v, axis=1, keepdims=True)


def col_sum(v):
    return jnp.sum(v, axis=0, keepdims=True)


def segments_of(position, first_end, second_end):
    return (position >= first_end).astype(jnp.int32) + (position >= second_end).astype(jnp.int32)


def decay_terms(dt_raw, hp_ref, rows):
    z = dt_raw + hp_ref[0:1, :]
    step = jnp.maximum(z, 0.0) + jnp.log1p(jnp.exp(-jnp.abs(z)))
    below = (iota((rows, rows), 1) <= iota((rows, rows), 0)).astype(F32)
    ld = dot_nn(below, step * (hp_ref[1:2, :] * LOG2E), HIGH)
    lr = ld - jnp.log2(jnp.maximum(step, 1e-37))
    return z, step, ld, lr


def to_rows(v, out_ref, pairs):
    vt = v.T
    for p in range(pairs):
        out_ref[p, 0:2, :] = vt[2 * p : 2 * p + 2, :]


def pair_lanes(ref, p):
    return pltpu.roll(ref[...], lax.rem(LANE - 2 * p, LANE), 1)


def ring_place(index, n):
    chip, core = index // 2, index % 2
    z, x = chip // 2, chip % 2
    return 2 * ((1 - x) * z + x * (n // 2 - 1 - z)) + core


def ring_device(place, n):
    spot, core = place // 2, place % 2
    far = spot // (n // 4)
    chip = (1 - far) * (2 * spot) + far * (2 * (n // 2 - 1 - spot) + 1)
    return 2 * chip + core


def tile_chunks(columns, parts):
    tiles = columns // LANE
    cuts = [LANE * (-(-tiles * i // parts)) for i in range(parts + 1)]
    return [(cuts[i], cuts[i + 1] - cuts[i]) for i in range(parts)]


def mixer_kernel(
    n, ring, ends, x_hbm, cot_hbm, win_hbm, wout_hbm, par_in, small_ref, hp_ref,
    out_hbm, ing_hbm, nin_hbm, nout_hbm, gproj_hbm, gbr_hbm, proj_hbm, csum_hbm, mixed_hbm,
    pack_ref, stat_ref,
    win, wout, xs, cot, recv, sent, nin, nout, gbr, gproj, proj, csum, mixed, wide_s, stage,
    act_bc, cols_s, rows_s, row_q, col_q, cb, dcb, maskb, stat, par_ref, small_got,
    load_sem, weight_sem, save_sem, store_sem, send_sem, recv_sem, hop_send, hop_recv, small_send, small_recv,
):
    section = lax.axis_index("section")
    me = lax.axis_index("dp")
    micros = x_hbm.shape[0]
    rows, d = nin.shape
    di, cw = mixed.shape[1], csum.shape[1]
    half = rows // 2
    pairs = di // LANE
    wide = proj.shape[1]
    lane = iota((rows, LANE), 1)
    first = lane < LANE // 2
    pos = iota((rows, LANE), 0)
    x_loads = [pltpu.make_async_copy(x_hbm.at[m], xs.at[m], load_sem.at[m]) for m in range(micros)]
    cot_loads = [
        pltpu.make_async_copy(cot_hbm.at[m], cot.at[m], load_sem.at[micros + m]) for m in range(micros)
    ]

    def tile(j, size):
        return pl.ds(pl.multiple_of(j * size, size), size)

    place = ring_place(me, n) if ring else 0
    steps = n // 2
    piece = win_hbm.shape[0]
    part = piece // 2
    targets = (ring_device((place + 1) % n, n), ring_device((place + n - 1) % n, n)) if ring else None
    shards_of = (win_hbm, wout_hbm)
    wholes = (win, wout)

    def own_load(which):
        if ring:
            to = wholes[which].at[tile(me, piece), :]
        else:
            to = wholes[which]
        return pltpu.make_async_copy(shards_of[which], to, weight_sem.at[which])

    def hop(which, way, k, c, sender):
        shift = n - k if way == 0 else k
        owner = ring_device((sender + shift) % n, n)
        rows_of = pl.ds(pl.multiple_of(owner * piece + c * part, part), part)
        return pltpu.make_async_remote_copy(
            src_ref=wholes[which].at[rows_of, :],
            dst_ref=wholes[which].at[rows_of, :],
            send_sem=hop_send.at[which, way, k, c],
            recv_sem=hop_recv.at[which, way, k, c],
            device_id=(section, targets[way]),
            device_id_type=pl.DeviceIdType.MESH,
        )

    def hop_arrived(which, way, k, c):
        hop(which, way, k, c, place + n - 1 if way == 0 else place + 1).wait_recv()

    def hops(which, k, start, take, last=False):
        for c in range(2):
            for way in range(2):
                if take:
                    hop_arrived(which, way, k - 1, c)
                if start and not (last and c != way):
                    hop(which, way, k, c, place).start()

    def hop_middle(which, low, high):
        repeat(high - low, lambda i: hops(which, low + i, True, True))

    def hop_end(which):
        for way in range(2):
            hop_arrived(which, way, steps - 1, way)

    def small_copy(source, target):
        return pltpu.make_async_remote_copy(
            src_ref=small_ref,
            dst_ref=small_got.at[source],
            send_sem=small_send.at[target],
            recv_sem=small_recv.at[source],
            device_id=(section, target),
            device_id_type=pl.DeviceIdType.MESH,
        )

    saves = [
        pltpu.make_async_copy(v, to, save_sem.at[i])
        for i, (v, to) in enumerate(((proj, proj_hbm), (csum, csum_hbm), (mixed, mixed_hbm)))
    ]
    restores = [
        pltpu.make_async_copy(to, v, save_sem.at[i])
        for i, (v, to) in enumerate(((proj, proj_hbm), (csum, csum_hbm), (mixed, mixed_hbm)))
    ]

    results = (
        (nin, nin_hbm), (nout, nout_hbm), (stage, out_hbm),
        (gbr, gbr_hbm), (gproj, gproj_hbm), (stage, ing_hbm),
    )

    def store(m, i):
        return pltpu.make_async_copy(results[i][0], results[i][1].at[m], store_sem.at[i])

    def hand_over(m, j):
        part = tile(j, OUT_TILE)
        return pltpu.make_async_remote_copy(
            src_ref=sent.at[m, :, part],
            dst_ref=recv.at[m, :, part],
            send_sem=send_sem.at[m, j],
            recv_sem=recv_sem.at[m, j],
            device_id=(1 - section, me),
            device_id_type=pl.DeviceIdType.MESH,
        )

    hands = d // OUT_TILE

    def repeat(count, body):
        def step(i, carry):
            body(i)
            return carry

        lax.fori_loop(0, count, step, 0)

    for copy in x_loads + cot_loads:
        copy.start()
    for which in range(2):
        own_load(which).start()
    recv[...] = jnp.zeros_like(recv)
    pack_ref[...] = jnp.zeros_like(pack_ref)
    stat_ref[...] = jnp.zeros_like(stat_ref)
    barrier = pltpu.get_barrier_semaphore()
    pl.semaphore_signal(barrier, inc=1, device_id=(1 - section, me), device_id_type=pl.DeviceIdType.MESH)
    if ring:

        def greet(i):
            pl.semaphore_signal(
                barrier,
                inc=1,
                device_id=(section, (me + i + 1) % n),
                device_id_type=pl.DeviceIdType.MESH,
            )

        repeat(n - 1, greet)
        pl.semaphore_wait(barrier, n)
        own_load(0).wait()
        hops(0, 0, True, False)
        repeat(n - 1, lambda i: small_copy(me, (me + i + 1) % n).start())
        hop_middle(0, 1, steps - 1)
        hops(0, steps - 1, True, True, True)
        own_load(1).wait()
        hops(1, 0, True, False)
        small_got[me] = small_ref[...]

        def small_take(i):
            other = (me + i + 1) % n
            small_copy(other, other).wait_recv()

        repeat(n - 1, small_take)
        tap_cols, gate_cols, pre_cols = (v.shape[1] // n for v in (csum, mixed, nin))
        joined = [small_got[o] for o in range(n)]
        par_ref[...] = par_in[...]
        par_ref[0:5, :] = jnp.concatenate([v[0:5, :tap_cols] for v in joined], axis=1)
        par_ref[5:6, :di] = jnp.concatenate([v[5:6, :gate_cols] for v in joined], axis=1)
        par_ref[7:8, :d] = jnp.concatenate([v[7:8, :pre_cols] for v in joined], axis=1)
        hop_end(0)

        @pl.when(section == 1)
        def _():
            hop_middle(1, 1, steps - 1)
            hops(1, steps - 1, True, True, True)
            hop_end(1)

    else:
        pl.semaphore_wait(barrier, 1)
        par_ref[...] = par_in[...]
        for which in range(2):
            own_load(which).wait()

    def early_hops(m, low, high):
        if ring and m == 0:

            @pl.when(section == 0)
            def _():
                hop_middle(1, low, min(high, steps - 1))
                if high == steps:
                    hops(1, steps - 1, True, True, True)
                    hop_end(1)

    def input_of(m, cols):
        u = xs[m, :, cols].astype(F32)
        return u + jnp.where(section == 1, recv[m, :, cols].astype(F32), 0.0)

    def set_mask(e1, e2, upper):
        rpos, cpos = iota((rows, rows), 0), iota((rows, rows), 1)
        keep = (rpos <= cpos) if upper else (rpos >= cpos)
        keep &= segments_of(rpos, e1, e2) == segments_of(cpos, e1, e2)
        maskb[...] = jnp.where(keep, 0.0, NEG)

    def forward(m):
        e1, e2 = ends[m, 0], ends[m, 1]
        x_loads[m].wait()

        @pl.when(section == 1)
        def _():
            repeat(hands, lambda j: hand_over(m, j).wait_recv())

        u = input_of(m, slice(None))
        q = lax.rsqrt(jnp.mean(u * u, axis=1, keepdims=True) + EPS)
        if m > 0:
            for copy in [store(m - 1, i) for i in range(3)] + saves:
                copy.wait()
        nin[...] = (u * q * par_ref[7:8, :d]).astype(BF16)
        store(m, 0).start()

        def project(c):
            proj[:, tile(c, IN_TILE)] = dot_nn(nin[...], win[:, tile(c, IN_TILE)])

        repeat(wide // IN_TILE, project)
        if m < micros - 1:
            saves[0].start()
        dist = pos - jnp.where(pos >= e2, e2, jnp.where(pos >= e1, e1, 0))

        def conv_tile(j):
            here = tile(j, LANE)
            v = proj[:, pl.ds(pl.multiple_of(di + j * LANE, LANE), LANE)]
            acc = par_ref[4:5, here] + par_ref[3:4, here] * v
            for lag in range(1, 4):
                acc += par_ref[3 - lag : 4 - lag, here] * jnp.where(
                    dist >= lag, pltpu.roll(v, lag, 0), 0.0
                )
            csum[:, here] = acc

        repeat(cw // LANE, conv_tile)
        early_hops(m, 1, 2)
        if m < micros - 1:
            saves[1].start()
        _, _, ld, lr = decay_terms(proj[:, di + cw :], hp_ref, rows)
        cols_s[...] = ld
        to_rows(lr, rows_s, pairs)
        for j in range(2):
            v = csum[:, di + j * LANE : di + (j + 1) * LANE]
            act_bc[j] = v * sigmoid(v)
        cb[...] = dot_nt(act_bc[1], act_bc[0], HIGH)
        set_mask(e1, e2, False)

        def pair(p, sq):
            here = tile(p, LANE)
            cs = csum[:, here]
            x = cs * sigmoid(cs)
            ldr = pair_lanes(cols_s, p)
            y0 = jnp.zeros((half, LANE), F32)
            y1 = jnp.zeros((half, LANE), F32)
            for h in range(2):
                xm = jnp.where(first if h == 0 else ~first, x, 0.0).astype(BF16)
                lc = ldr[:, h : h + 1]
                lrow = rows_s[p, h : h + 1, :]
                m0 = jnp.exp2((lc[:half] - lrow[:, :half]) + maskb[:half, :half]) * cb[:half, :half]
                m1 = jnp.exp2((lc[half:] - lrow) + maskb[half:, :]) * cb[half:, :]
                y0 += dot_nn(m0.astype(BF16), xm[:half])
                y1 += dot_nn(m1.astype(BF16), xm)
            y = jnp.concatenate([y0, y1], axis=0) + par_ref[6:7, here] * x
            mixed[:, here] = y
            gate = proj[:, here]
            g = y * (gate * sigmoid(gate))
            wide_s[:, here] = g
            return sq + g * g

        sq = lax.fori_loop(0, pairs // 2, pair, jnp.zeros((rows, LANE), F32))
        early_hops(m, 2, 3)
        sq = lax.fori_loop(pairs // 2, pairs, pair, sq)
        early_hops(m, 3, 4)
        if m < micros - 1:
            saves[2].start()
        r = lax.rsqrt(row_sum(sq) * (1.0 / di) + EPS)
        nout[...] = (wide_s[...] * r * par_ref[5:6, :di]).astype(BF16)
        store(m, 1).start()
        early_hops(m, 4, steps)
        valid = iota((rows, 1), 0) < e2

        def branch_tile(j):
            here = tile(j, OUT_TILE)
            branch = dot_nt(nout[...], wout[here, :])
            u = input_of(m, here)
            stage[:, here] = u + branch

            @pl.when(section == 0)
            def _():
                sent[m, :, here] = branch.astype(BF16)
                hand_over(m, j).start()

            usq = col_sum(row_sum(jnp.where(valid, u * u, 0.0)))
            bsq = col_sum(row_sum(jnp.where(valid, branch * branch, 0.0)))
            at = iota((8, LANE), 1)
            stat_ref[...] += jnp.where(at == 0, usq, jnp.where(at == 1, bsq, 0.0))

        repeat(hands, branch_tile)
        store(m, 2).start()

    def backward(m):
        e1, e2 = ends[m, 0], ends[m, 1]
        newest = m == micros - 1

        @pl.when(section == 0)
        def _():
            repeat(hands, lambda j: hand_over(m, j).wait_recv())

        cot_loads[m].wait()
        valid = (iota((rows, 1), 0) < e2).astype(F32)
        if not newest:
            store(m + 1, 3).wait()
        gbr[...] = jnp.where(
            section == 1, cot[m].astype(F32) * valid, recv[m].astype(F32)
        ).astype(BF16)
        store(m, 3).start()
        if not newest:
            for copy in restores:
                copy.wait()

        def gate_tile(c, carry):
            gn = dot_nn(gbr[...], wout[:, tile(c, IN_TILE)])
            wide_s[:, tile(c, IN_TILE)] = gn
            sq, cross = carry
            for j in range(IN_TILE // LANE):
                here = pl.ds(pl.multiple_of(c * IN_TILE + j * LANE, LANE), LANE)
                gate = proj[:, here]
                gated = mixed[:, here] * (gate * sigmoid(gate))
                sq += gated * gated
                cross += gated * (par_ref[5:6, here] * gn[:, j * LANE : (j + 1) * LANE])
            return sq, cross

        zero = jnp.zeros((rows, LANE), F32)
        sq, cross = lax.fori_loop(0, di // IN_TILE, gate_tile, (zero, zero))
        r = lax.rsqrt(row_sum(sq) * (1.0 / di) + EPS)
        rc = r * r * r * (row_sum(cross) * (1.0 / di))
        stat[0] = jnp.broadcast_to(r, (rows, LANE))
        stat[1] = jnp.broadcast_to(rc, (rows, LANE))
        z, dt, ld, lr = decay_terms(proj[:, di + cw :], hp_ref, rows)
        cols_s[...] = lr
        to_rows(ld, rows_s, pairs)
        for j in range(2):
            v = csum[:, di + j * LANE : di + (j + 1) * LANE]
            act_bc[j] = v * sigmoid(v)
        cb[...] = dot_nt(act_bc[0], act_bc[1], HIGH)
        set_mask(e1, e2, True)
        dcb[...] = jnp.zeros_like(dcb)
        col_q[...] = jnp.zeros_like(col_q)
        ahead = jnp.where(pos < e1, e1, jnp.where(pos < e2, e2, rows)) - pos
        if not newest:
            store(m + 1, 4).wait()

        def conv_back(dcv, off):
            here = pl.ds(off, LANE)
            there = pl.ds(pl.multiple_of(di + off, LANE), LANE)
            v = proj[:, there]
            out = par_ref[3:4, here] * dcv
            pack_ref[3:4, here] += col_sum(dcv * v)
            pack_ref[4:5, here] += col_sum(dcv)
            for lag in range(1, 4):
                moved = jnp.where(ahead > lag, pltpu.roll(dcv, rows - lag, 0), 0.0)
                out += par_ref[3 - lag : 4 - lag, here] * moved
                pack_ref[3 - lag : 4 - lag, here] += col_sum(moved * v)
            gproj[:, there] = out.astype(BF16)

        def pair(p):
            off = pl.multiple_of(p * LANE, LANE)
            here = pl.ds(off, LANE)
            gate = proj[:, here]
            mx = mixed[:, here]
            gnt = wide_s[:, here]
            sg = sigmoid(gate)
            sil = gate * sg
            gated = mx * sil
            pack_ref[5:6, here] += col_sum(gated * stat[0] * gnt)
            gg = stat[0] * (par_ref[5:6, here] * gnt) - gated * stat[1]
            dy = gg * sil
            gproj[:, here] = (gg * mx * (sg * (1.0 + gate * (1.0 - sg)))).astype(BF16)
            cs = csum[:, here]
            sc = sigmoid(cs)
            x = cs * sc
            pack_ref[6:7, here] += col_sum(dy * x)
            xb = x.astype(BF16)
            lrr = pair_lanes(cols_s, p)
            dx0 = jnp.zeros((half, LANE), F32)
            dx1 = jnp.zeros((half, LANE), F32)
            for h in range(2):
                dym = jnp.where(first if h == 0 else ~first, dy, 0.0).astype(BF16)
                lc = lrr[:, h : h + 1]
                lrow = rows_s[p, h : h + 1, :]
                d0 = jnp.exp2((lrow - lc[:half]) + maskb[:half, :])
                d1 = jnp.exp2((lrow[:, half:] - lc[half:]) + maskb[half:, half:])
                t0 = dot_nt(xb[:half], dym) * d0
                t1 = dot_nt(xb[half:], dym[half:]) * d1
                dx0 += dot_nn((d0 * cb[:half, :]).astype(BF16), dym)
                dx1 += dot_nn((d1 * cb[half:, half:]).astype(BF16), dym[half:])
                dcb[:half, :] += t0
                dcb[half:, half:] += t1
                q0 = t0 * cb[:half, :]
                q1 = t1 * cb[half:, half:]
                row_q[p, h : h + 1, :half] = col_sum(q0[:, :half])
                row_q[p, h : h + 1, half:] = col_sum(q0[:, half:]) + col_sum(q1)
                picked = lane == 2 * p + h
                col_q[:half, :] = jnp.where(picked[:half], row_sum(q0), col_q[:half, :])
                col_q[half:, :] = jnp.where(picked[half:], row_sum(q1), col_q[half:, :])
            dx = jnp.concatenate([dx0, dx1], axis=0) + par_ref[6:7, here] * dy
            conv_back(dx * (sc * (1.0 + cs * (1.0 - sc))), off)

        repeat(pairs, pair)
        total = dcb[...]
        for j, grad in enumerate((dot_nn(total, act_bc[1], HIGH), dot_tn(total, act_bc[0], HIGH))):
            cs = csum[:, di + j * LANE : di + (j + 1) * LANE]
            sc = sigmoid(cs)
            conv_back(grad * (sc * (1.0 + cs * (1.0 - sc))), di + j * LANE)
        spread = jnp.concatenate(
            [row_q[p, 0:2, :] for p in range(pairs)]
            + [jnp.zeros((LANE - 2 * pairs, rows), F32)],
            axis=0,
        )
        colq = col_q[...]
        above = (iota((rows, rows), 1) >= iota((rows, rows), 0)).astype(F32)
        after = dot_nn(above, spread.T - colq, HIGH)
        sz = sigmoid(z)
        ratio = jnp.where(z < -20.0, 1.0, sz / jnp.maximum(dt, 1e-37))
        neg_rate = hp_ref[1:2, :]
        ddt = jnp.where(lane < 2 * pairs, colq * ratio + neg_rate * after * sz, 0.0)
        gproj[:, di + cw :] = ddt.astype(BF16)
        pack_ref[7:8, d : d + LANE] += col_sum(ddt)
        pack_ref[7:8, d + LANE : d + 2 * LANE] += col_sum(
            jnp.where(lane < 2 * pairs, neg_rate * dt * after, 0.0)
        )
        store(m, 4).start()
        if m > 0:
            for copy in restores:
                copy.start()
        if newest:
            store(m, 2).wait()
        else:
            store(m + 1, 5).wait()

        def back_tile(j):
            stage[:, tile(j, OUT_TILE)] = dot_nt(gproj[...], win[tile(j, OUT_TILE), :])

        repeat(hands, back_tile)
        u = input_of(m, slice(None))
        q = lax.rsqrt(jnp.mean(u * u, axis=1, keepdims=True) + EPS)
        gi = stage[...]
        uq3 = q * q * q * jnp.mean(u * (par_ref[7:8, :d] * gi), axis=1, keepdims=True)
        pack_ref[7:8, :d] += col_sum(u * q * gi)

        def end_tile(j):
            here = tile(j, OUT_TILE)
            grad = (
                gbr[:, here].astype(F32)
                + q * (par_ref[7:8, here] * stage[:, here])
                - input_of(m, here) * uq3
            )
            stage[:, here] = grad

            @pl.when(section == 1)
            def _():
                sent[m, :, here] = grad.astype(BF16)
                hand_over(m, j).start()

        repeat(hands, end_tile)
        store(m, 5).start()

    for m in range(micros):
        forward(m)
    for i in range(2):
        store(micros - 1, i).wait()
    for m in reversed(range(micros)):
        backward(m)
    for i in range(3, 6):
        store(0, i).wait()
    for m in range(micros):
        repeat(hands, lambda j: hand_over(m, j).wait_send())
    if ring:
        for which in range(2):
            for way in range(2):
                for c in range(2):
                    count = steps if c == way else steps - 1
                    repeat(count, lambda k: hop(which, way, k, c, place).wait_send())

        def small_sent(i):
            small_copy(me, (me + i + 1) % n).wait_send()

        repeat(n - 1, small_sent)


def mixer_steps(n, ring, ends, x_in, cot, w_in, w_out_t, par, small, hp):
    micros, rows, d = x_in.shape
    di = w_out_t.shape[1]
    wide = w_in.shape[1]
    cw = par.shape[1]
    pairs = di // LANE
    steps = n // 2
    hands = d // OUT_TILE
    hbm = pl.BlockSpec(memory_space=pl.ANY)
    vmem = pl.BlockSpec(memory_space=pltpu.VMEM)

    def stack(width, dtype):
        return jax.ShapeDtypeStruct((micros, rows, width), dtype)

    return pl.pallas_call(
        functools.partial(mixer_kernel, n, ring),
        in_specs=[pl.BlockSpec(memory_space=pltpu.SMEM)] + [hbm] * 4 + [vmem] * 3,
        out_specs=[hbm] * 9 + [vmem] * 2,
        out_shape=[
            stack(d, F32), stack(d, F32), stack(d, BF16), stack(di, BF16), stack(wide, BF16), stack(d, BF16),
            jax.ShapeDtypeStruct((rows, wide), F32),
            jax.ShapeDtypeStruct((rows, cw), F32),
            jax.ShapeDtypeStruct((rows, di), F32),
            jax.ShapeDtypeStruct((8, cw), F32),
            jax.ShapeDtypeStruct((8, LANE), F32),
        ],
        scratch_shapes=[
            pltpu.VMEM((d, wide), BF16),
            pltpu.VMEM((d, di), BF16),
            pltpu.VMEM((micros, rows, d), BF16),
            pltpu.VMEM((micros, rows, d), BF16),
            pltpu.VMEM((micros, rows, d), BF16),
            pltpu.VMEM((micros, rows, d), BF16),
            pltpu.VMEM((rows, d), BF16),
            pltpu.VMEM((rows, di), BF16),
            pltpu.VMEM((rows, d), BF16),
            pltpu.VMEM((rows, wide), BF16),
            pltpu.VMEM((rows, wide), F32),
            pltpu.VMEM((rows, cw), F32),
            pltpu.VMEM((rows, di), F32),
            pltpu.VMEM((rows, di), F32),
            pltpu.VMEM((rows, d), F32),
            pltpu.VMEM((2, rows, LANE), F32),
            pltpu.VMEM((rows, LANE), F32),
            pltpu.VMEM((pairs, 8, rows), F32),
            pltpu.VMEM((pairs, 8, rows), F32),
            pltpu.VMEM((rows, LANE), F32),
            pltpu.VMEM((rows, rows), F32),
            pltpu.VMEM((rows, rows), F32),
            pltpu.VMEM((rows, rows), F32),
            pltpu.VMEM((2, rows, LANE), F32),
            pltpu.VMEM(par.shape, F32),
            pltpu.VMEM((n, *small.shape), F32),
            pltpu.SemaphoreType.DMA((2 * micros,)),
            pltpu.SemaphoreType.DMA((2,)),
            pltpu.SemaphoreType.DMA((3,)),
            pltpu.SemaphoreType.DMA((6,)),
            pltpu.SemaphoreType.DMA((micros, hands)),
            pltpu.SemaphoreType.DMA((micros, hands)),
            pltpu.SemaphoreType.DMA((2, 2, steps, 2)),
            pltpu.SemaphoreType.DMA((2, 2, steps, 2)),
            pltpu.SemaphoreType.DMA((n,)),
            pltpu.SemaphoreType.DMA((n,)),
        ],
        compiler_params=pltpu.CompilerParams(
            collective_id=1, has_side_effects=True, vmem_limit_bytes=MIXER_VMEM
        ),
        cost_estimate=pl.CostEstimate(
            flops=12 * rows * d * (wide + di), bytes_accessed=100 << 20, transcendentals=16 << 20
        ),
        name="mixer_steps",
    )(ends, x_in, cot, w_in, w_out_t, par, small, hp)


def greet_all(n, me, section):
    barrier = pltpu.get_barrier_semaphore()

    def signal(i, carry):
        pl.semaphore_signal(
            barrier, inc=1, device_id=(section, (me + i) % n), device_id_type=pl.DeviceIdType.MESH
        )
        return carry

    lax.fori_loop(1, n, signal, 0)
    pl.semaphore_wait(barrier, n - 1)


def scatter_kernel(
    n, nin_t, gbr_t, gproj_hbm, nout_hbm, small_ref,
    gin_ref, gout_ref, small_out,
    gproj, nout, held, small_got, load_sem, send_sem, recv_sem, small_send, small_recv,
):
    me = lax.axis_index("dp")
    section = lax.axis_index("section")
    place = ring_place(me, n)
    steps = n // 2
    micros, rows = gproj_hbm.shape[0], gproj_hbm.shape[1]
    wide, di = gproj.shape[1], nout.shape[1]
    targets = (ring_device((place + 1) % n, n), ring_device((place + n - 1) % n, n))
    loads = []
    for m in range(micros):
        part = pl.ds(m * rows, rows)
        loads.append(pltpu.make_async_copy(nout_hbm.at[m], nout.at[part], load_sem.at[0, m]))
        loads.append(pltpu.make_async_copy(gproj_hbm.at[m], gproj.at[part], load_sem.at[1, m]))
    for load in loads:
        load.start()
    greet_all(n, me, section)

    def small_copy(other, slot):
        return pltpu.make_async_remote_copy(
            src_ref=small_ref.at[other],
            dst_ref=small_got.at[slot],
            send_sem=small_send.at[slot],
            recv_sem=small_recv.at[slot],
            device_id=(section, other),
            device_id_type=pl.DeviceIdType.MESH,
        )

    def small_start(i, carry):
        small_copy((me + i) % n, i).start()
        return carry

    lax.fori_loop(1, n, small_start, 0)
    for load in loads:
        load.wait()

    out_cuts = tile_chunks(di, 2)
    in_cuts = tile_chunks(wide, 4)
    chunks = [
        (False, *out_cuts[0]), (False, *out_cuts[1]),
        (True, *in_cuts[0]), (True, *in_cuts[2]), (True, *in_cuts[1]), (True, *in_cuts[3]),
    ]

    def own(owner, chunk):
        is_in, start, size = chunk
        if is_in:
            return dot_nn(nin_t[owner], gproj[:, start : start + size])
        return dot_nn(gbr_t[owner], nout[:, start : start + size])

    def columns(chunk):
        is_in, start, size = chunk
        return pl.ds(start if is_in else wide + start, size)

    def owner_of(way, k):
        shift = steps - k if way == 0 else n - steps + k
        return ring_device((place + shift) % n, n)

    def send(way, k, c):
        cols = columns(chunks[c])
        return pltpu.make_async_remote_copy(
            src_ref=held.at[way, k, :, cols],
            dst_ref=held.at[way, k + 1, :, cols],
            send_sem=send_sem.at[way, k, c],
            recv_sem=recv_sem.at[way, k, c],
            device_id=(section, targets[way]),
            device_id_type=pl.DeviceIdType.MESH,
        )

    def run_step(k, first, second):
        for c, chunk in enumerate(chunks):
            for way in range(2):
                if first and c % 2 != way:
                    continue
                cols = columns(chunk)
                total = own(owner_of(way, k), chunk)
                if not first and not (second and c % 2 != way):
                    send(way, k - 1, c).wait_recv()
                    total += held[way, k, :, cols].astype(F32)
                held[way, k, :, cols] = total.astype(BF16)
                send(way, k, c).start()

    run_step(0, True, False)
    run_step(1, False, True)

    def loop(k, carry):
        run_step(k, False, False)
        return carry

    lax.fori_loop(2, steps, loop, 0)

    for c, chunk in enumerate(chunks):
        is_in, start, size = chunk
        cols = columns(chunk)
        total = own(me, chunk)
        for way in range(2):
            send(way, steps - 1, c).wait_recv()
            total += held[way, steps, :, cols].astype(F32)
        if is_in:
            gin_ref[:, start : start + size] = total
        else:
            gout_ref[:, start : start + size] = total

    small_out[...] = small_ref[me]

    def small_end(i, carry):
        copy = small_copy((me + i) % n, i)
        copy.wait()
        small_out[...] += small_got[i]
        return carry

    lax.fori_loop(1, n, small_end, 0)
    for c in range(len(chunks)):
        send(c % 2, 0, c).wait_send()

    def sent(k, carry):
        for c in range(len(chunks)):
            for way in range(2):
                send(way, k, c).wait_send()
        return carry

    lax.fori_loop(1, steps, sent, 0)


def scatter_gradients(n, nin_t, gbr_t, gproj, nout, small):
    piece, tokens = nin_t.shape[1:]
    wide, di = gproj.shape[2], nout.shape[2]
    micros = nout.shape[0]
    steps = n // 2
    vmem = pl.BlockSpec(memory_space=pltpu.VMEM)
    hbm = pl.BlockSpec(memory_space=pl.ANY)
    return pl.pallas_call(
        functools.partial(scatter_kernel, n),
        out_shape=[
            jax.ShapeDtypeStruct((piece, wide), F32),
            jax.ShapeDtypeStruct((piece, di), F32),
            jax.ShapeDtypeStruct(small.shape[1:], F32),
        ],
        in_specs=[vmem, vmem, hbm, hbm, vmem],
        out_specs=[vmem, vmem, vmem],
        scratch_shapes=[
            pltpu.VMEM((tokens, wide), BF16),
            pltpu.VMEM((tokens, di), BF16),
            pltpu.VMEM((2, steps + 1, piece, wide + di), BF16),
            pltpu.VMEM(small.shape, F32),
            pltpu.SemaphoreType.DMA((2, micros)),
            pltpu.SemaphoreType.DMA((2, steps, 6)),
            pltpu.SemaphoreType.DMA((2, steps, 6)),
            pltpu.SemaphoreType.DMA((n,)),
            pltpu.SemaphoreType.DMA((n,)),
        ],
        compiler_params=pltpu.CompilerParams(
            collective_id=0, has_side_effects=True, vmem_limit_bytes=VMEM_LIMIT
        ),
        cost_estimate=pl.CostEstimate(
            flops=2 * n * piece * tokens * (wide + di), bytes_accessed=20 << 20, transcendentals=0
        ),
        name="gradient_scatter",
    )(nin_t, gbr_t, gproj, nout, small)


def shards(
    x_in, lengths, norm_pre, w_in, conv_w, conv_b, dt_bias, a_log, skip_scale, norm_gate, w_out, cotangent
):
    micros, rows, d = x_in.shape
    heads = dt_bias.shape[1]
    taps = conv_w.shape[1]
    devices = lax.axis_size("dp")
    piece, wide = w_in.shape[1], w_in.shape[2]
    di = w_out.shape[1]
    cw_piece, gate_piece = conv_w.shape[2], norm_gate.shape[1]
    cw = cw_piece * devices
    pad = LANE - heads

    ring = piece % 32 == 0 and devices % 4 == 0 and devices >= 12
    skip_row = jnp.repeat(skip_scale[0], di // heads)

    def wide_row(v, width):
        return jnp.pad(v, (0, width - v.shape[0]))[None]

    if ring:
        shard_in = jnp.pad(w_in[0], ((0, 0), (0, pad)))
        shard_out = w_out[0].T
        small = jnp.concatenate(
            [
                conv_w[0],
                conv_b,
                wide_row(norm_gate[0], cw_piece),
                jnp.zeros((1, cw_piece), BF16),
                wide_row(norm_pre[0], cw_piece),
            ],
            axis=0,
        ).astype(F32)
        small = jnp.pad(small, ((0, 0), (0, -cw_piece % LANE)))
        par = jnp.pad(skip_row[None], ((6, 1), (0, cw - di)))
    else:
        small = jnp.concatenate([norm_pre[0], conv_b[0], norm_gate[0], conv_w[0].reshape(-1)])
        small = jnp.pad(small, (0, piece * pad - small.shape[0])).reshape(piece, pad)
        shard_in = lax.all_gather(jnp.concatenate([w_in[0], small], axis=1), "dp", axis=0, tiled=True)
        shard_out = lax.all_gather(w_out[0].T, "dp", axis=0, tiled=True)
        tails = shard_in[:, wide:].reshape(devices, piece * pad).astype(F32)
        cuts = [0]
        for size in (piece, cw_piece, gate_piece, taps * cw_piece):
            cuts.append(cuts[-1] + size)
        conv_taps = tails[:, cuts[3] : cuts[4]].reshape(devices, taps, cw_piece)
        par = jnp.concatenate(
            [
                conv_taps.transpose(1, 0, 2).reshape(taps, cw),
                tails[:, cuts[1] : cuts[2]].reshape(1, -1),
                wide_row(tails[:, cuts[2] : cuts[3]].reshape(-1), cw),
                wide_row(skip_row, cw),
                wide_row(tails[:, cuts[0] : cuts[1]].reshape(-1), cw),
            ],
            axis=0,
        )
        small = jnp.zeros((8, LANE), F32)
    hp = jnp.pad(jnp.stack([dt_bias[0], -jnp.exp(a_log[0])]), ((0, 6), (0, pad)))

    first_end = lengths[:, 0, 0]
    second_end = first_end + lengths[:, 0, 1]
    ends = jnp.stack([first_end, second_end], axis=1)
    (outputs, in_grad, normed_in, normed_out, grad_proj, grad_branch, _, _, _, packs, stats) = mixer_steps(
        devices, ring, ends, x_in, cotangent, shard_in, shard_out, par, small, hp
    )
    valid_total = jnp.sum(second_end).astype(F32)

    def turned(v):
        return v.reshape(micros * rows, d).T.reshape(devices, piece, micros * rows)

    me = lax.axis_index("dp")
    per_head = packs[6, :di].reshape(heads, di // heads).sum(axis=1)
    common = jnp.concatenate(
        [
            packs[7, d : d + heads],
            packs[7, d + LANE : d + LANE + heads],
            per_head,
            stats[0, :2],
            valid_total[None],
        ]
    )
    small = jnp.concatenate(
        [
            packs[:taps].reshape(taps, devices, cw_piece).transpose(1, 0, 2).reshape(devices, -1),
            packs[4].reshape(devices, cw_piece),
            packs[5, :di].reshape(devices, gate_piece),
            packs[7, :d].reshape(devices, piece),
            jnp.broadcast_to(common, (devices, common.shape[0])),
        ],
        axis=1,
    )
    small_rows = -(-small.shape[1] // (8 * LANE)) * 8
    small = jnp.pad(small, ((0, 0), (0, small_rows * LANE - small.shape[1])))
    in_shard, out_shard, small = scatter_gradients(
        devices, turned(normed_in), turned(grad_branch), grad_proj, normed_out,
        small.reshape(devices, small_rows, LANE),
    )
    small = small.reshape(-1)
    parts = []
    start = 0
    for size in (taps * cw_piece, cw_piece, gate_piece, piece, heads, heads, heads, 3):
        parts.append(small[start : start + size])
        start += size
    sums = parts[7]
    rms = jnp.sqrt(sums[:2] / (sums[2] * d))

    return (
        outputs[None],
        in_grad[None],
        parts[3][None],
        in_shard[None, :, :wide],
        parts[0].reshape(1, taps, cw_piece),
        parts[1][None],
        parts[4][None],
        parts[5][None],
        parts[6][None],
        parts[2][None],
        out_shard.T[None],
        rms[None],
    )


def solution(mesh):
    placed = (
        P(None, "dp", None),
        P(None, "dp", None),
        P("section", "dp"),
        P("section", "dp", None),
        P("section", None, "dp"),
        P("section", "dp"),
        P("section", None),
        P("section", None),
        P("section", None),
        P("section", "dp"),
        P("section", None, "dp"),
        P(None, "dp", None),
    )
    return jax.shard_map(
        shards,
        mesh=mesh,
        in_specs=placed,
        out_specs=(
            P("section", None, "dp", None),
            P("section", None, "dp", None),
            P("section", "dp"),
            P("section", "dp", None),
            P("section", None, "dp"),
            P("section", "dp"),
            P("section", None),
            P("section", None),
            P("section", None),
            P("section", "dp"),
            P("section", None, "dp"),
            P("section", None),
        ),
        check_vma=False,
    )
```
